128 devices in a mesh: row: 8 (over y, x_lo), col: 16 (over x_hi, z, core).
Axes of the slice: x: 4 (x_hi: 2, x_lo: 2; x = x_hi * 2 + x_lo), y: 4, z: 4, core: 2. Of those that a mesh axis runs over, the one named last changes fastest.
Arguments:
- vectors: float32 [32768, 128], P(('row', 'col')), may hold values from -6 to 6
- widths: int32 [256], P(('row', 'col')), may hold values from 64 to 128, as said below
- tiles: bfloat16 [8, 16, 256, 128, 128], P('row', 'col'), may hold values from -0.03125 to 0.03125
- block_rows: int32 [8, 16, 256], P('row', 'col'), may hold values from 0 to 31, as said below
- block_cols: int32 [8, 16, 256], P('row', 'col'), may hold values from 0 to 15
- block_count: int32 [8, 16], P('row', 'col'), may hold values from 64 to 256, as said below
Outputs:
- filtered: float32 [32768, 128], P(('row', 'col'))
The draws below stay inside these ranges and needn't reach their ends.
Inputs may be any that keep to these rules, and one draw needn't show every extreme that they name: `widths`: every atom has a width from 64 to 128; both ends occur. `block_rows`: used slots of one tile name distinct blocks (a, b) of global atom row a and column b; a block is stored only where a <= b with a + b even, or a > b with a + b odd, so each mirror pair is stored at most once. `block_count`: some tile uses all 256 slots and some tile 256 // 4.
All inputs are finite; a program needn't handle non-finite values.
Results may differ from the reference program's by a relative error of at most 0.0042.
Values may be sent and summed in bfloat16 or wider, within the bound.
No kernel may reach another device: no remote copies, remote signals or barrier semaphores. Data moves between devices by JAX's collectives and lax.ppermute only.
A program may use at most 128 MiB of HBM per device.

```python
import jax
import jax.numpy as jnp
from jax import lax

ATOM = 128
VECS = 128
AR = 32
AC = 16
SLOTS = 256
NA = 256
NROWS = 32768
N_ROW = 8
N_COL = 16


def block_pattern(key):
    positions = AR * AC
    score_key, count_key, full_key, least_key = jax.random.split(key, 4)
    scores = jax.random.randint(score_key, (N_ROW, N_COL, positions), 0, 2 ** 14)
    place = jnp.arange(positions, dtype=jnp.int32)
    local_row = place // AC
    local_col = place % AC
    grid_row = jnp.arange(N_ROW, dtype=jnp.int32)[:, None, None]
    grid_col = jnp.arange(N_COL, dtype=jnp.int32)[None, :, None]
    atom_row = grid_row * AR + local_row[None, None, :]
    atom_col = grid_col * AC + local_col[None, None, :]
    parity_even = (atom_row + atom_col) % 2 == 0
    allowed = jnp.where(parity_even, atom_row <= atom_col, atom_row > atom_col)
    ranked = jnp.where(allowed, scores * 65536 + place[None, None, :], -1 - place[None, None, :])
    chosen = lax.top_k(ranked, SLOTS)[1].astype(jnp.int32)
    tiles_all = N_ROW * N_COL
    counts = jax.random.randint(count_key, (tiles_all,), SLOTS // 4, SLOTS + 1)
    full_spot = jax.random.randint(full_key, (), 0, tiles_all)
    least_spot = (full_spot + 1 + jax.random.randint(least_key, (), 0, tiles_all - 1)) % tiles_all
    counts = counts.at[full_spot].set(SLOTS).at[least_spot].set(SLOTS // 4)
    return (chosen // AC, chosen % AC, counts.reshape(N_ROW, N_COL).astype(jnp.int32))


def draw_block_rows(key, part):
    return block_pattern(key)[0]


def draw_block_cols(key, part):
    return block_pattern(key)[1]


def draw_block_count(key, part):
    return block_pattern(key)[2]


def draw_widths(key, part):
    key = jax.random.fold_in(key, 7)
    first_key, second_key, third_key = jax.random.split(key, 3)
    values = jax.random.randint(first_key, (NA,), ATOM // 2, ATOM + 1)
    low_spot = jax.random.randint(second_key, (), 0, NA)
    high_spot = (low_spot + 1 + jax.random.randint(third_key, (), 0, NA - 1)) % NA
    values = values.at[low_spot].set(ATOM // 2).at[high_spot].set(ATOM)
    return values.astype(jnp.int32)


def steps_of(key, shape, pieces, low, top_value):
    def one(dim, parts):
        draws = jax.random.uniform(jax.random.fold_in(jax.random.fold_in(key, 6), dim), (parts,), jnp.float32, low / len(pieces), top_value / len(pieces))
        return jnp.repeat(jnp.exp(draws), shape[dim] // parts).reshape((-1,) + (1,) * (len(shape) - dim - 1))

    level = one(*pieces[0])
    for cut in pieces[1:]:
        level = level * one(*cut)
    return level


def noise(key, extent, spread, most, pieces=(), held_as=jnp.bfloat16):
    factor_of = steps_of(key, extent, pieces, -0.22, 0.18) if pieces else 1.0
    entries = jax.random.normal(key, extent, jnp.float32) * spread * factor_of
    return jnp.minimum(jnp.maximum(entries, -most), most).astype(held_as)


def setup_inputs(seed: int = 0) -> dict:
    key_list = jax.random.split(jax.random.key(seed), 7)
    vectors = noise(key_list[0], (NROWS, VECS), 1.0, 6.0, ((0, 128),), jnp.float32)
    widths = draw_widths(jax.random.fold_in(key_list[6], 71), 0)
    tiles = noise(key_list[2], (N_ROW, N_COL, SLOTS, ATOM, ATOM), NROWS ** -0.5, 0.03125, ((0, 8), (1, 16)))
    block_rows = draw_block_rows(jax.random.fold_in(key_list[6], 71), 0)
    block_cols = draw_block_cols(jax.random.fold_in(key_list[6], 71), 0)
    block_count = draw_block_count(jax.random.fold_in(key_list[6], 71), 0)
    return {"vectors": vectors, "widths": widths, "tiles": tiles, "block_rows": block_rows, "block_cols": block_cols, "block_count": block_count}


center = 0.25


def apply_matrix(current, tiles, block_rows, block_cols, block_count, row_keep):
    rounded = lax.optimization_barrier(current.astype(jnp.bfloat16)).astype(jnp.float32)
    blocks_in = rounded.reshape(AR * N_ROW, ATOM, VECS)

    def tile_step(total, items):
        tile_set, rows_here, cols_here, count_here, position = items
        grid_row = position // N_COL
        grid_col = position % N_COL
        global_rows = (grid_row * AR + rows_here).astype(jnp.int32)
        global_cols = (grid_col * AC + cols_here).astype(jnp.int32)
        live_slots = (jnp.arange(SLOTS) < count_here).astype(jnp.float32)[:, None, None]
        tile_float = tile_set.astype(jnp.float32)
        direct = jnp.einsum("sab,sbk->sak", tile_float, blocks_in[global_cols]) * live_slots
        mirror = jnp.einsum("sab,sak->sbk", tile_float, blocks_in[global_rows]) * live_slots
        total = total.at[global_rows].add(direct).at[global_cols].add(mirror)
        return total, None

    items = (tiles.reshape(N_ROW * N_COL, SLOTS, ATOM, ATOM),
             block_rows.reshape(N_ROW * N_COL, SLOTS),
             block_cols.reshape(N_ROW * N_COL, SLOTS),
             block_count.reshape(N_ROW * N_COL),
             jnp.arange(N_ROW * N_COL, dtype=jnp.int32))
    start = jnp.zeros((AR * N_ROW, ATOM, VECS), jnp.float32)
    total, unused = lax.scan(tile_step, start, items)
    return total.reshape(AR * N_ROW * ATOM, VECS) * row_keep


def reference(vectors, widths, tiles, block_rows, block_cols, block_count):
    row_keep = (jnp.arange(ATOM)[None, :] < widths[:, None]).astype(jnp.float32).reshape(-1, 1)
    first = vectors * row_keep
    second = apply_matrix(first, tiles, block_rows, block_cols, block_count, row_keep) - center * first
    third = apply_matrix(second, tiles, block_rows, block_cols, block_count, row_keep)
    return 2.0 * (third - center * second) - first
```

```python
import functools

import jax
import jax.numpy as jnp
from jax import lax
from jax.experimental import pallas as pl
from jax.experimental.pallas import tpu as pltpu
from jax.sharding import Mesh
from jax.sharding import PartitionSpec as P

CENTER = 0.25
ATOM = 128
VECS = 128
AR = 32
AC = 16
SLOTS = 256
N_ROW = 8
N_COL = 16
BF = jnp.bfloat16
F32 = jnp.float32
ROWS = ("y", "xl")
COLS = ("xh", "z", "co")
ALL = ROWS + COLS
D_LEN = 9
M_LEN = 17


def tables(slot_rows, slot_cols, count, row, col):
    place = jnp.where(jnp.arange(SLOTS) < count, slot_rows * AC + slot_cols, -1)

    def pack(rows, cols, index, zero):
        want = (rows * AC + cols).reshape(-1, 1)
        entry = jnp.arange(SLOTS)[None, :] * 64 + index.reshape(-1, 1) - zero
        return zero + jnp.sum(jnp.where(place[None, :] == want, entry, 0), axis=1)

    a = jnp.arange(AR)[:, None]
    q = jnp.arange(D_LEN)[None, :]
    ga = row * AR + a
    gb = col * AC + 2 * q
    odd = ga % 2 == 1
    main = 2 * q + jnp.where(odd, ga <= gb + 1, ga > gb).astype(jnp.int32)
    extra = ga - 1 - col * AC
    extra = jnp.where(odd & (extra >= 0) & (extra < AC), extra, -AC * AR)
    b = jnp.where(q < 8, main, extra)
    direct = pack(a + 0 * b, b, b, AC)

    b = jnp.arange(AC)[:, None]
    q = jnp.arange(M_LEN)[None, :]
    gb = col * AC + b
    ga = row * AR + 2 * q
    odd = gb % 2 == 1
    main = 2 * q + jnp.where(odd, ga + 1 <= gb, ga > gb).astype(jnp.int32)
    extra = gb + 1 - row * AR
    extra = jnp.where((~odd) & (extra >= 0) & (extra < AR), extra, -AR)
    a = jnp.where(q < 16, main, extra)
    mirror = pack(a, b + 0 * a, a, AR)
    return direct, mirror


def direct_kernel(tab, core, x_ref, t_ref, mine_ref, other_ref, held):
    held[:AC] = x_ref[...].reshape(AC, ATOM, VECS)
    held[AC] = jnp.zeros((ATOM, VECS), BF)
    co = core[0]

    def product(a, q, n):
        blocks, xs = [], []
        for k in range(n):
            e = tab[a * D_LEN + q + k]
            blocks.append(t_ref[lax.shift_right_logical(e, 6)])
            xs.append(held[jnp.bitwise_and(e, 63)])
        if n == 1:
            left, right = blocks[0], xs[0]
        else:
            left, right = jnp.concatenate(blocks, 1), jnp.concatenate(xs, 0)
        return jnp.dot(left, right, preferred_element_type=F32)

    def step(xz, carry):
        for which, out in ((0, mine_ref), (1, other_ref)):
            for t in range(2):
                a = 4 * xz + 2 * (co if which == 0 else 1 - co) + t
                total = product(a, 0, 8)
                if t:
                    total = total + product(a, 8, 1)
                out[xz, t * ATOM:(t + 1) * ATOM, :] = total.astype(out.dtype)
        return carry

    lax.fori_loop(0, 8, step, 0)


def mirror_kernel(tab, x_ref, y_ref, core, t_ref, out_ref, held):
    co = core[0]
    for xz in range(8):
        held[pl.ds(4 * xz + 2 * co, 2)] = x_ref[xz]
        held[pl.ds(4 * xz + 2 - 2 * co, 2)] = y_ref[xz]
    held[AR] = jnp.zeros((VECS, ATOM), BF)

    def product(b, q, n):
        blocks, xs = [], []
        for k in range(n):
            e = tab[b * M_LEN + q + k]
            blocks.append(t_ref[lax.shift_right_logical(e, 6)])
            xs.append(held[jnp.bitwise_and(e, 63)])
        if n == 1:
            left, right = xs[0], blocks[0]
        else:
            left, right = jnp.concatenate(xs, 1), jnp.concatenate(blocks, 0)
        return jnp.dot(left, right, preferred_element_type=F32)

    def step(k, carry):
        for t in range(2):
            b = 2 * k + t
            total = product(b, 0, 8) + product(b, 8, 8)
            if not t:
                total = total + product(b, 16, 1)
            out_ref[k, t] = total.astype(out_ref.dtype)
        return carry

    lax.fori_loop(0, 8, step, 0)


SMEM = pl.BlockSpec(memory_space=pltpu.SMEM)
VMEM = pl.BlockSpec(memory_space=pltpu.VMEM)
PARAMS = pltpu.CompilerParams(vmem_limit_bytes=32 * 1024 * 1024)


def direct_call(tab, core, x, tiles):
    return pl.pallas_call(
        direct_kernel,
        out_shape=(
            jax.ShapeDtypeStruct((8, 2 * ATOM, VECS), F32),
            jax.ShapeDtypeStruct((8, 2 * ATOM, VECS), BF),
        ),
        in_specs=[SMEM, SMEM, VMEM, VMEM],
        out_specs=(VMEM, VMEM),
        scratch_shapes=[pltpu.VMEM((AC + 1, ATOM, VECS), BF)],
        compiler_params=PARAMS,
        cost_estimate=pl.CostEstimate(
            flops=2 * SLOTS * ATOM**3, bytes_accessed=2**23, transcendentals=0
        ),
        name="direct",
    )(tab, core, x, tiles)


def mirror_call(tab, core, x, y, tiles):
    return pl.pallas_call(
        mirror_kernel,
        out_shape=jax.ShapeDtypeStruct((8, 2, VECS, ATOM), BF),
        in_specs=[SMEM, VMEM, VMEM, SMEM, VMEM],
        out_specs=VMEM,
        scratch_shapes=[pltpu.VMEM((AR + 1, VECS, ATOM), BF)],
        compiler_params=PARAMS,
        cost_estimate=pl.CostEstimate(
            flops=2 * SLOTS * ATOM**3, bytes_accessed=2**23, transcendentals=0
        ),
        name="mirror",
    )(tab, x, y, core, tiles)


TO_COL = [(r * 16 + c, (c % 8) * 16 + 2 * r + c // 8) for r in range(8) for c in range(16)]
TO_ROW = [(d, s) for s, d in TO_COL]
SWAP = [(0, 1), (1, 0)]


def local(vectors, widths, tiles, block_rows, block_cols, block_count):
    row = lax.axis_index(ROWS)
    col = lax.axis_index(COLS)
    core = lax.axis_index("co").astype(jnp.int32).reshape(1)
    tile_set = tiles[0, 0]
    direct_tab, mirror_tab = tables(
        block_rows[0, 0], block_cols[0, 0], block_count[0, 0], row, col
    )
    keep = (jnp.arange(ATOM)[None, :] < widths[:, None]).astype(F32).reshape(2 * ATOM, 1)

    def flip(x):
        return x.reshape(2, ATOM, VECS).swapaxes(1, 2)

    def copies(x):
        return jnp.broadcast_to(x[None], (8, *x.shape))

    def exchange(x, axes):
        return lax.all_to_all(x, axes, split_axis=0, concat_axis=0, tiled=True)

    def apply_matrix(current):
        rounded = current.astype(BF)
        piece = lax.ppermute(rounded, ALL, TO_COL)
        near = exchange(copies(flip(rounded)), ("xh", "z"))
        far = lax.ppermute(near, "co", SWAP)
        piece, near = lax.optimization_barrier((piece, near))
        col_block = exchange(copies(piece), ROWS)
        mirror = mirror_call(mirror_tab, core, near, far, tile_set)
        mine, other = direct_call(direct_tab, core, col_block, tile_set)
        theirs = lax.ppermute(other, "co", SWAP)
        got = exchange(mirror, ROWS)
        got = flip(jnp.sum(got.astype(F32), axis=0)).reshape(2 * ATOM, VECS)
        back = lax.ppermute(got.astype(BF), ALL, TO_ROW)
        both = (mine + theirs.astype(F32)).astype(BF)
        own = jnp.sum(exchange(both, ("xh", "z")).astype(F32), axis=0)
        return (own + back.astype(F32)) * keep

    first = vectors * keep
    second = apply_matrix(first) - CENTER * first
    third = apply_matrix(second)
    return 2.0 * (third - CENTER * second) - first


def solution(mesh):
    split = Mesh(mesh.devices.reshape(4, 2, 2, 4, 2), ALL)
    return jax.shard_map(
        local,
        mesh=split,
        in_specs=(
            P(ALL, None),
            P(ALL),
            P(ROWS, COLS, None, None, None),
            P(ROWS, COLS, None),
            P(ROWS, COLS, None),
            P(ROWS, COLS),
        ),
        out_specs=P(ALL, None),
        check_vma=False,
    )
```

```python
import functools

import jax
import jax.numpy as jnp
from jax import lax
from jax.experimental import pallas as pl
from jax.experimental.pallas import tpu as pltpu
from jax.sharding import Mesh
from jax.sharding import PartitionSpec as P

CENTER = 0.25
ATOM = 128
VECS = 128
AR = 32
AC = 16
SLOTS = 256
N_ROW = 8
N_COL = 16
BF = jnp.bfloat16
F32 = jnp.float32
ROWS = ("y", "xl")
COLS = ("xh", "z", "co")
ALL = ROWS + COLS
D_LEN = 9
M_LEN = 17


def tables(slot_rows, slot_cols, count, row, col):
    place = jnp.where(jnp.arange(SLOTS) < count, slot_rows * AC + slot_cols, -1)

    def pack(rows, cols, index, zero):
        want = (rows * AC + cols).reshape(-1, 1)
        entry = jnp.arange(SLOTS)[None, :] * 64 + index.reshape(-1, 1) - zero
        return zero + jnp.sum(jnp.where(place[None, :] == want, entry, 0), axis=1)

    a = jnp.arange(AR)[:, None]
    q = jnp.arange(D_LEN)[None, :]
    ga = row * AR + a
    gb = col * AC + 2 * q
    odd = ga % 2 == 1
    main = 2 * q + jnp.where(odd, ga <= gb + 1, ga > gb).astype(jnp.int32)
    extra = ga - 1 - col * AC
    extra = jnp.where(odd & (extra >= 0) & (extra < AC), extra, -AC * AR)
    b = jnp.where(q < 8, main, extra)
    direct = pack(a + 0 * b, b, b, AC)

    b = jnp.arange(AC)[:, None]
    q = jnp.arange(M_LEN)[None, :]
    gb = col * AC + b
    ga = row * AR + 2 * q
    odd = gb % 2 == 1
    main = 2 * q + jnp.where(odd, ga + 1 <= gb, ga > gb).astype(jnp.int32)
    extra = gb + 1 - row * AR
    extra = jnp.where((~odd) & (extra >= 0) & (extra < AR), extra, -AR)
    a = jnp.where(q < 16, main, extra)
    mirror = pack(a, b + 0 * a, a, AR)
    return direct, mirror


def keep_of(widths, shape, axis):
    place = lax.broadcasted_iota(jnp.int32, shape, axis)
    atom = lax.broadcasted_iota(jnp.int32, shape, 0)
    return (place < jnp.where(atom == 0, widths[0], widths[1])).astype(F32)


def send_forms(current, plain_ref, flip_ref):
    plain_ref[...] = current.reshape(2 * ATOM, VECS).astype(BF)
    flipped = jnp.swapaxes(current, 1, 2).astype(BF)
    for k in range(8):
        flip_ref[k] = flipped


def first_kernel(widths, vectors_ref, plain_ref, flip_ref):
    shape = (2, ATOM, VECS)
    first = vectors_ref[...].reshape(shape) * keep_of(widths, shape, 1)
    send_forms(first, plain_ref, flip_ref)


def applied(widths, own_ref, near_ref, far_ref):
    shape = (2, ATOM, VECS)
    total = near_ref[...] + far_ref[...]
    for k in range(8):
        total = total + own_ref[k].astype(F32)
    return total.reshape(shape) * keep_of(widths, shape, 1)


def second_kernel(widths, own_ref, near_ref, far_ref, vectors_ref, out_ref, plain_ref, flip_ref):
    shape = (2, ATOM, VECS)
    first = vectors_ref[...].reshape(shape) * keep_of(widths, shape, 1)
    second = applied(widths, own_ref, near_ref, far_ref) - CENTER * first
    out_ref[...] = second.reshape(2 * ATOM, VECS)
    send_forms(second, plain_ref, flip_ref)


def last_kernel(widths, own_ref, near_ref, far_ref, vectors_ref, second_ref, out_ref):
    shape = (2, ATOM, VECS)
    first = vectors_ref[...].reshape(shape) * keep_of(widths, shape, 1)
    third = applied(widths, own_ref, near_ref, far_ref)
    out = 2.0 * (third - CENTER * second_ref[...].reshape(shape)) - first
    out_ref[...] = out.reshape(2 * ATOM, VECS)


def load_kernel(src_ref, out_ref, sem):
    copy = pltpu.make_async_copy(src_ref, out_ref, sem)
    copy.start()
    copy.wait()


def direct_kernel(tab, place, x0_ref, x1_ref, x2_ref, x3_ref, t_ref, mine_ref, other_ref, held):
    co, y, xl = place[0], place[1], place[2]
    for s, ref in enumerate((x0_ref, x1_ref, x2_ref, x3_ref)):
        for rel in range(2):
            k = 2 * jnp.bitwise_and(y - s + 4, 3) + jnp.bitwise_xor(xl, rel)
            held[pl.ds(2 * k, 2)] = ref[rel].reshape(2, ATOM, VECS)
    held[AC] = jnp.zeros((ATOM, VECS), BF)

    def product(a, q, n):
        blocks, xs = [], []
        for k in range(n):
            e = tab[a * D_LEN + q + k]
            blocks.append(t_ref[lax.shift_right_logical(e, 6)])
            xs.append(held[jnp.bitwise_and(e, 63)])
        if n == 1:
            left, right = blocks[0], xs[0]
        else:
            left, right = jnp.concatenate(blocks, 1), jnp.concatenate(xs, 0)
        return jnp.dot(left, right, preferred_element_type=F32)

    def step(xz, carry):
        for which, out in ((0, mine_ref), (1, other_ref)):
            for t in range(2):
                a = 4 * xz + 2 * (co if which == 0 else 1 - co) + t
                total = product(a, 0, 8)
                if t:
                    total = total + product(a, 8, 1)
                out[xz, t * ATOM:(t + 1) * ATOM, :] = total.astype(out.dtype)
        return carry

    lax.fori_loop(0, 8, step, 0)


def mirror_kernel(tab, place, x_ref, y_ref, t_ref, o0_ref, o1_ref, o2_ref, o3_ref, held):
    co, y, xl = place[0], place[1], place[2]
    for xz in range(8):
        held[pl.ds(4 * xz + 2 * co, 2)] = x_ref[xz]
        held[pl.ds(4 * xz + 2 - 2 * co, 2)] = y_ref[xz]
    held[AR] = jnp.zeros((VECS, ATOM), BF)

    def product(b, q, n):
        blocks, xs = [], []
        for k in range(n):
            e = tab[b * M_LEN + q + k]
            blocks.append(t_ref[lax.shift_right_logical(e, 6)])
            xs.append(held[jnp.bitwise_and(e, 63)])
        if n == 1:
            left, right = xs[0], blocks[0]
        else:
            left, right = jnp.concatenate(xs, 1), jnp.concatenate(blocks, 0)
        return jnp.dot(left, right, preferred_element_type=F32)

    for s, out in enumerate((o0_ref, o1_ref, o2_ref, o3_ref)):

        def step(rel, carry, s=s, out=out):
            k = 2 * jnp.bitwise_and(y + s, 3) + jnp.bitwise_xor(xl, rel)
            for t in range(2):
                b = 2 * k + t
                total = product(b, 0, 8) + product(b, 8, 8)
                if not t:
                    total = total + product(b, 16, 1)
                out[rel, t] = total.astype(out.dtype)
            return carry

        lax.fori_loop(0, 2, step, 0)


def gathered_kernel(o0_ref, o1_ref, o2_ref, o3_ref, near_ref, far_ref):
    for rel, out in enumerate((near_ref, far_ref)):
        total = o0_ref[rel] + o1_ref[rel].astype(F32) + o2_ref[rel].astype(F32) + o3_ref[rel].astype(F32)
        out[...] = jnp.swapaxes(total, 1, 2).reshape(2 * ATOM, VECS)


def both_kernel(mine_ref, theirs_ref, out_ref):
    out_ref[...] = (mine_ref[...] + theirs_ref[...]).astype(BF)


SMEM = pl.BlockSpec(memory_space=pltpu.SMEM)
VMEM = pl.BlockSpec(memory_space=pltpu.VMEM)
PARAMS = pltpu.CompilerParams(vmem_limit_bytes=24 * 1024 * 1024)
PIECE = (2 * ATOM, VECS)
BLOCKS = (2, ATOM, VECS)


def like(shape, dtype):
    return jax.ShapeDtypeStruct(shape, dtype)


def call(kernel, out_shape, scalars, arrays, scratch=(), flops=0, size=2**20, name=None):
    single = not isinstance(out_shape, tuple)
    return pl.pallas_call(
        kernel,
        out_shape=out_shape,
        in_specs=[SMEM] * len(scalars) + [VMEM] * len(arrays),
        out_specs=VMEM if single else (VMEM,) * len(out_shape),
        scratch_shapes=list(scratch),
        compiler_params=PARAMS,
        cost_estimate=pl.CostEstimate(flops=flops, bytes_accessed=size, transcendentals=0),
        name=name,
    )(*scalars, *arrays)


def load(tiles):
    return pl.pallas_call(
        load_kernel,
        out_shape=pltpu.VMEM(tiles.shape, tiles.dtype),
        in_specs=[pl.BlockSpec(memory_space=pl.ANY)],
        scratch_shapes=[pltpu.SemaphoreType.DMA],
        compiler_params=pltpu.CompilerParams(vmem_limit_bytes=2**20),
        cost_estimate=pl.CostEstimate(flops=0, bytes_accessed=2**23, transcendentals=0),
        name="load",
    )(tiles)


def pairs(rel):
    return [
        (r * 16 + c, ((c % 8) ^ rel) * 16 + 2 * r + c // 8) for r in range(8) for c in range(16)
    ]


SWAP = [(0, 1), (1, 0)]


def turn(s):
    return [(k, (k + s) % 4) for k in range(4)]


def local(vectors, widths, tiles, block_rows, block_cols, block_count):
    row = lax.axis_index(ROWS)
    col = lax.axis_index(COLS)
    place = jnp.stack([lax.axis_index(n) for n in ("co", "y", "xl")]).astype(jnp.int32)
    tile_set = tiles[0, 0]
    direct_tab, mirror_tab = tables(
        block_rows[0, 0], block_cols[0, 0], block_count[0, 0], row, col
    )
    work = dict(flops=2 * SLOTS * ATOM**3, size=2**22)

    def exchange(x):
        return lax.all_to_all(x, ("xh", "z"), split_axis=0, concat_axis=0, tiled=True)

    def apply_matrix(plain, flipped):
        piece = jnp.stack([lax.ppermute(plain, ALL, pairs(rel)) for rel in range(2)])
        near = exchange(flipped)
        xs = [piece] + [lax.ppermute(piece, "y", turn(s)) for s in (1, 2, 3)]
        far = lax.ppermute(near, "co", SWAP)
        mine, other = call(
            direct_kernel,
            (like((8, *PIECE), F32), like((8, *PIECE), F32)),
            (direct_tab, place),
            (*xs, tile_set),
            [pltpu.VMEM((AC + 1, ATOM, VECS), BF)],
            name="direct",
            **work,
        )
        theirs = lax.ppermute(other, "co", SWAP)
        near, mine = lax.optimization_barrier((near, mine))
        outs = call(
            mirror_kernel,
            (like((2, *BLOCKS), F32),) + (like((2, *BLOCKS), BF),) * 3,
            (mirror_tab, place),
            (near, far, tile_set),
            [pltpu.VMEM((AR + 1, VECS, ATOM), BF)],
            name="mirror",
            **work,
        )
        both = call(both_kernel, like((8, *PIECE), BF), (), (mine, theirs), name="both")
        own = exchange(both)
        outs = [outs[0]] + [lax.ppermute(outs[s], "y", turn(s)) for s in (1, 2, 3)]
        sums = call(
            gathered_kernel, (like(PIECE, F32), like(PIECE, F32)), (), tuple(outs), name="gathered"
        )
        back = [
            lax.ppermute(sums[rel], ALL, [(d, s) for s, d in pairs(rel)]) for rel in range(2)
        ]
        return own, back[0], back[1]

    forms = (like(PIECE, BF), like((8, *BLOCKS), BF))
    plain, flipped = call(first_kernel, forms, (widths,), (vectors,), name="first")
    parts = apply_matrix(plain, flipped)
    second, plain, flipped = call(
        second_kernel, (like(PIECE, F32), *forms), (widths,), (*parts, vectors), name="second"
    )
    parts = apply_matrix(plain, flipped)
    return call(
        last_kernel, like(PIECE, F32), (widths,), (*parts, vectors, second), name="last"
    )

def solution(mesh):
    split = Mesh(mesh.devices.reshape(4, 2, 2, 4, 2), ALL)
    return jax.shard_map(
        local,
        mesh=split,
        in_specs=(
            P(ALL, None),
            P(ALL),
            P(ROWS, COLS, None, None, None),
            P(ROWS, COLS, None),
            P(ROWS, COLS, None),
            P(ROWS, COLS),
        ),
        out_specs=P(ALL, None),
        check_vma=False,
    )
```

```python
import functools

import jax
import jax.numpy as jnp
from jax import lax
from jax.experimental import pallas as pl
from jax.experimental.pallas import tpu as pltpu
from jax.sharding import Mesh
from jax.sharding import PartitionSpec as P

CENTER = 0.25
ATOM = 128
VECS = 128
AR = 32
AC = 16
SLOTS = 256
N_ROW = 8
N_COL = 16
BF = jnp.bfloat16
F32 = jnp.float32
ROWS = ("y", "xl")
COLS = ("xh", "z", "co")
ALL = ROWS + COLS
D_LEN = 9
M_LEN = 17


def tables(slot_rows, slot_cols, count, row, col):
    place = jnp.where(jnp.arange(SLOTS) < count, slot_rows * AC + slot_cols, -1)

    def pack(rows, cols, index, zero):
        want = (rows * AC + cols).reshape(-1, 1)
        entry = jnp.arange(SLOTS)[None, :] * 64 + index.reshape(-1, 1) - zero
        return zero + jnp.sum(jnp.where(place[None, :] == want, entry, 0), axis=1)

    a = jnp.arange(AR)[:, None]
    q = jnp.arange(D_LEN)[None, :]
    ga = row * AR + a
    gb = col * AC + 2 * q
    odd = ga % 2 == 1
    main = 2 * q + jnp.where(odd, ga <= gb + 1, ga > gb).astype(jnp.int32)
    extra = ga - 1 - col * AC
    extra = jnp.where(odd & (extra >= 0) & (extra < AC), extra, -AC * AR)
    b = jnp.where(q < 8, main, extra)
    direct = pack(a + 0 * b, b, b, AC)

    b = jnp.arange(AC)[:, None]
    q = jnp.arange(M_LEN)[None, :]
    gb = col * AC + b
    ga = row * AR + 2 * q
    odd = gb % 2 == 1
    main = 2 * q + jnp.where(odd, ga + 1 <= gb, ga > gb).astype(jnp.int32)
    extra = gb + 1 - row * AR
    extra = jnp.where((~odd) & (extra >= 0) & (extra < AR), extra, -AR)
    a = jnp.where(q < 16, main, extra)
    mirror = pack(a, b + 0 * a, a, AR)
    return direct, mirror


def keep_of(widths, shape, axis):
    place = lax.broadcasted_iota(jnp.int32, shape, axis)
    atom = lax.broadcasted_iota(jnp.int32, shape, 0)
    return (place < jnp.where(atom == 0, widths[0], widths[1])).astype(F32)


def send_forms(current, plain_ref, flip_ref):
    plain_ref[...] = current.reshape(2 * ATOM, VECS).astype(BF)
    flipped = jnp.swapaxes(current, 1, 2).astype(BF)
    for k in range(8):
        flip_ref[k] = flipped


def first_kernel(widths, vectors_ref, plain_ref, flip_ref):
    shape = (2, ATOM, VECS)
    first = vectors_ref[...].reshape(shape) * keep_of(widths, shape, 1)
    send_forms(first, plain_ref, flip_ref)


def applied(widths, own_ref, back_ref):
    shape = (2, ATOM, VECS)
    total = back_ref[...]
    for k in range(8):
        total = total + own_ref[k].astype(F32)
    return total.reshape(shape) * keep_of(widths, shape, 1)


def second_kernel(widths, own_ref, back_ref, vectors_ref, out_ref, plain_ref, flip_ref):
    shape = (2, ATOM, VECS)
    first = vectors_ref[...].reshape(shape) * keep_of(widths, shape, 1)
    second = applied(widths, own_ref, back_ref) - CENTER * first
    out_ref[...] = second.reshape(2 * ATOM, VECS)
    send_forms(second, plain_ref, flip_ref)


def last_kernel(widths, own_ref, back_ref, vectors_ref, second_ref, out_ref):
    shape = (2, ATOM, VECS)
    first = vectors_ref[...].reshape(shape) * keep_of(widths, shape, 1)
    third = applied(widths, own_ref, back_ref)
    out = 2.0 * (third - CENTER * second_ref[...].reshape(shape)) - first
    out_ref[...] = out.reshape(2 * ATOM, VECS)


def piece_at(place, i):
    y, xl = i // 2, i % 2
    return 2 * jnp.bitwise_and(y - place[1] + 4, 3) + xl


def direct_kernel(tab, place, x_ref, t_ref, mine_ref, other_ref, held):
    co = place[0]
    for i in range(8):
        held[pl.ds(2 * piece_at(place, i), 2)] = x_ref[i].reshape(2, ATOM, VECS)
    held[AC] = jnp.zeros((ATOM, VECS), BF)

    def product(a, q, n):
        blocks, xs = [], []
        for k in range(n):
            e = tab[a * D_LEN + q + k]
            blocks.append(t_ref[lax.shift_right_logical(e, 6)])
            xs.append(held[jnp.bitwise_and(e, 63)])
        if n == 1:
            left, right = blocks[0], xs[0]
        else:
            left, right = jnp.concatenate(blocks, 1), jnp.concatenate(xs, 0)
        return jnp.dot(left, right, preferred_element_type=F32)

    def step(xz, carry):
        for which, out in ((0, mine_ref), (1, other_ref)):
            for t in range(2):
                a = 4 * xz + 2 * (co if which == 0 else 1 - co) + t
                total = product(a, 0, 8)
                if t:
                    total = total + product(a, 8, 1)
                out[xz, t * ATOM:(t + 1) * ATOM, :] = total.astype(out.dtype)
        return carry

    lax.fori_loop(0, 8, step, 0)


def mirror_kernel(tab, place, x_ref, y_ref, t_ref, out_ref, held):
    co = place[0]
    for xz in range(8):
        held[pl.ds(4 * xz + 2 * co, 2)] = x_ref[xz]
        held[pl.ds(4 * xz + 2 - 2 * co, 2)] = y_ref[xz]
    held[AR] = jnp.zeros((VECS, ATOM), BF)

    def product(b, q, n):
        blocks, xs = [], []
        for k in range(n):
            e = tab[b * M_LEN + q + k]
            blocks.append(t_ref[lax.shift_right_logical(e, 6)])
            xs.append(held[jnp.bitwise_and(e, 63)])
        if n == 1:
            left, right = xs[0], blocks[0]
        else:
            left, right = jnp.concatenate(xs, 1), jnp.concatenate(blocks, 0)
        return jnp.dot(left, right, preferred_element_type=F32)

    def step(i, carry):
        k = piece_at(place, i)
        for t in range(2):
            b = 2 * k + t
            total = product(b, 0, 8) + product(b, 8, 8)
            if not t:
                total = total + product(b, 16, 1)
            out_ref[i, t] = total.astype(out_ref.dtype)
        return carry

    lax.fori_loop(0, 8, step, 0)


def gathered_kernel(got_ref, out_ref):
    total = got_ref[0].astype(F32)
    for i in range(1, 8):
        total = total + got_ref[i].astype(F32)
    out_ref[...] = jnp.swapaxes(total, 1, 2).reshape(2 * ATOM, VECS)


def both_kernel(mine_ref, theirs_ref, out_ref):
    out_ref[...] = (mine_ref[...] + theirs_ref[...].astype(F32)).astype(BF)


SMEM = pl.BlockSpec(memory_space=pltpu.SMEM)
VMEM = pl.BlockSpec(memory_space=pltpu.VMEM)
PARAMS = pltpu.CompilerParams(vmem_limit_bytes=24 * 1024 * 1024)
PIECE = (2 * ATOM, VECS)
BLOCKS = (2, ATOM, VECS)


def like(shape, dtype):
    return jax.ShapeDtypeStruct(shape, dtype)


def call(kernel, out_shape, scalars, arrays, scratch=(), flops=0, size=2**20, name=None):
    single = not isinstance(out_shape, tuple)
    return pl.pallas_call(
        kernel,
        out_shape=out_shape,
        in_specs=[SMEM] * len(scalars) + [VMEM] * len(arrays),
        out_specs=VMEM if single else (VMEM,) * len(out_shape),
        scratch_shapes=list(scratch),
        compiler_params=PARAMS,
        cost_estimate=pl.CostEstimate(flops=flops, bytes_accessed=size, transcendentals=0),
        name=name,
    )(*scalars, *arrays)


def shift_of(column):
    r = column // 2
    return (r // 2 - r % 4 + 2 * (column % 2)) % 4


def owners(r, c):
    column = 2 * r + c // 8
    y, xl = (c % 8 // 2 + shift_of(column)) % 4, c % 2
    return (2 * y + xl) * 16 + column


TO_COL = [(r * 16 + c, owners(r, c)) for r in range(8) for c in range(16)]
TO_ROW = [(d, s) for s, d in TO_COL]
SWAP = [(0, 1), (1, 0)]


def local(vectors, widths, tiles, block_rows, block_cols, block_count):
    row = lax.axis_index(ROWS)
    col = lax.axis_index(COLS)
    place = jnp.stack([lax.axis_index("co"), shift_of(col)]).astype(jnp.int32)
    tile_set = tiles[0, 0]
    direct_tab, mirror_tab = tables(
        block_rows[0, 0], block_cols[0, 0], block_count[0, 0], row, col
    )
    work = dict(flops=2 * SLOTS * ATOM**3, size=2**23)

    def exchange(x, axes):
        return lax.all_to_all(x, axes, split_axis=0, concat_axis=0, tiled=True)

    def apply_matrix(plain, flipped):
        piece = lax.ppermute(plain, ALL, TO_COL)
        near = exchange(flipped, ("xh", "z"))
        far = lax.ppermute(near, "co", SWAP)
        piece, near = lax.optimization_barrier((piece, near))
        col_block = exchange(jnp.broadcast_to(piece[None], (8, *PIECE)), ROWS)
        mirror = call(
            mirror_kernel,
            like((8, *BLOCKS), BF),
            (mirror_tab, place),
            (near, far, tile_set),
            [pltpu.VMEM((AR + 1, VECS, ATOM), BF)],
            name="mirror",
            **work,
        )
        col_block, mirror = lax.optimization_barrier((col_block, mirror))
        got = exchange(mirror, ROWS)
        mine, other = call(
            direct_kernel,
            (like((8, *PIECE), F32), like((8, *PIECE), BF)),
            (direct_tab, place),
            (col_block, tile_set),
            [pltpu.VMEM((AC + 1, ATOM, VECS), BF)],
            name="direct",
            **work,
        )
        other, got = lax.optimization_barrier((other, got))
        theirs = lax.ppermute(other, "co", SWAP)
        both = call(both_kernel, like((8, *PIECE), BF), (), (mine, theirs), name="both")
        own = exchange(both, ("xh", "z"))
        gathered = call(gathered_kernel, like(PIECE, F32), (), (got,), name="gathered")
        back = lax.ppermute(gathered, ALL, TO_ROW)
        return own, back

    forms = (like(PIECE, BF), like((8, *BLOCKS), BF))
    plain, flipped = call(first_kernel, forms, (widths,), (vectors,), name="first")
    parts = apply_matrix(plain, flipped)
    second, plain, flipped = call(
        second_kernel, (like(PIECE, F32), *forms), (widths,), (*parts, vectors), name="second"
    )
    parts = apply_matrix(plain, flipped)
    return call(
        last_kernel, like(PIECE, F32), (widths,), (*parts, vectors, second), name="last"
    )

def solution(mesh):
    split = Mesh(mesh.devices.reshape(4, 2, 2, 4, 2), ALL)
    return jax.shard_map(
        local,
        mesh=split,
        in_specs=(
            P(ALL, None),
            P(ALL),
            P(ROWS, COLS, None, None, None),
            P(ROWS, COLS, None),
            P(ROWS, COLS, None),
            P(ROWS, COLS),
        ),
        out_specs=P(ALL, None),
        check_vma=False,
    )
```

```python
import functools

import jax
import jax.numpy as jnp
from jax import lax
from jax.experimental import pallas as pl
from jax.experimental.pallas import tpu as pltpu
from jax.sharding import Mesh
from jax.sharding import PartitionSpec as P

CENTER = 0.25
ATOM = 128
VECS = 128
AR = 32
AC = 16
SLOTS = 256
N_ROW = 8
N_COL = 16
BF = jnp.bfloat16
F32 = jnp.float32
ROWS = ("y", "xl")
COLS = ("xh", "z", "co")
ALL = ROWS + COLS
D_LEN = 9
M_LEN = 17


def tables(slot_rows, slot_cols, count, row, col):
    place = jnp.where(jnp.arange(SLOTS) < count, slot_rows * AC + slot_cols, -1)

    def pack(rows, cols, index, zero):
        want = (rows * AC + cols).reshape(-1, 1)
        entry = jnp.arange(SLOTS)[None, :] * 64 + index.reshape(-1, 1) - zero
        return zero + jnp.sum(jnp.where(place[None, :] == want, entry, 0), axis=1)

    a = jnp.arange(AR)[:, None]
    q = jnp.arange(D_LEN)[None, :]
    ga = row * AR + a
    gb = col * AC + 2 * q
    odd = ga % 2 == 1
    main = 2 * q + jnp.where(odd, ga <= gb + 1, ga > gb).astype(jnp.int32)
    extra = ga - 1 - col * AC
    extra = jnp.where(odd & (extra >= 0) & (extra < AC), extra, -AC * AR)
    b = jnp.where(q < 8, main, extra)
    direct = pack(a + 0 * b, b, b, AC)

    b = jnp.arange(AC)[:, None]
    q = jnp.arange(M_LEN)[None, :]
    gb = col * AC + b
    ga = row * AR + 2 * q
    odd = gb % 2 == 1
    main = 2 * q + jnp.where(odd, ga + 1 <= gb, ga > gb).astype(jnp.int32)
    extra = gb + 1 - row * AR
    extra = jnp.where((~odd) & (extra >= 0) & (extra < AR), extra, -AR)
    a = jnp.where(q < 16, main, extra)
    mirror = pack(a, b + 0 * a, a, AR)
    return direct, mirror


def keep_of(widths, shape, axis):
    place = lax.broadcasted_iota(jnp.int32, shape, axis)
    atom = lax.broadcasted_iota(jnp.int32, shape, 0)
    return (place < jnp.where(atom == 0, widths[0], widths[1])).astype(F32)


def send_forms(current, plain_ref, flip_ref):
    plain_ref[...] = current.reshape(2 * ATOM, VECS).astype(BF)
    flipped = jnp.swapaxes(current, 1, 2).astype(BF)
    for k in range(8):
        flip_ref[k] = flipped


def first_kernel(widths, vectors_ref, plain_ref, flip_ref):
    shape = (2, ATOM, VECS)
    first = vectors_ref[...].reshape(shape) * keep_of(widths, shape, 1)
    send_forms(first, plain_ref, flip_ref)


def applied(widths, own_ref, back_ref):
    shape = (2, ATOM, VECS)
    total = back_ref[...]
    for k in range(8):
        total = total + own_ref[k].astype(F32)
    return total.reshape(shape) * keep_of(widths, shape, 1)


def second_kernel(widths, own_ref, back_ref, vectors_ref, out_ref, plain_ref, flip_ref):
    shape = (2, ATOM, VECS)
    first = vectors_ref[...].reshape(shape) * keep_of(widths, shape, 1)
    second = applied(widths, own_ref, back_ref) - CENTER * first
    out_ref[...] = second.reshape(2 * ATOM, VECS)
    send_forms(second, plain_ref, flip_ref)


def last_kernel(widths, own_ref, back_ref, vectors_ref, second_ref, out_ref):
    shape = (2, ATOM, VECS)
    first = vectors_ref[...].reshape(shape) * keep_of(widths, shape, 1)
    third = applied(widths, own_ref, back_ref)
    out = 2.0 * (third - CENTER * second_ref[...].reshape(shape)) - first
    out_ref[...] = out.reshape(2 * ATOM, VECS)


def piece_at(place, i):
    y, xl = i // 2, i % 2
    return 2 * jnp.bitwise_and(y - place[1] + 4, 3) + xl


def streamed(steps, fetch, wait, compute):
    fetch(0)
    fetch(1)

    def step(n, carry):
        fetch(n + 2)
        wait(n)
        compute(n)
        return carry

    lax.fori_loop(0, steps - 2, step, 0)
    for n in (steps - 2, steps - 1):
        wait(n)
        compute(n)


def direct_kernel(far, tab, place, x_ref, t_ref, out_ref, held, blocks, sem):
    for i in range(8):
        held[pl.ds(2 * piece_at(place, i), 2)] = x_ref[i].reshape(2, ATOM, VECS)
    held[AC] = jnp.zeros((ATOM, VECS), BF)
    core = 1 - place[0] if far else place[0]

    def entry(n, q):
        return tab[(4 * n + 2 * core) * D_LEN + q + (1 if q >= 8 else 0)]

    def fetch(n):
        for q in range(17):
            source = t_ref.at[lax.shift_right_logical(entry(n, q), 6)]
            pltpu.make_async_copy(source, blocks.at[n, q], sem.at[n]).start()

    def wait(n):
        pltpu.make_async_copy(t_ref.at[pl.ds(0, 17)], blocks.at[n], sem.at[n]).wait()

    def compute(n):
        for t, (low, high) in enumerate(((0, 8), (8, 17))):
            left = jnp.concatenate([blocks[n, q] for q in range(low, high)], 1)
            right = [held[jnp.bitwise_and(entry(n, q), 63)] for q in range(low, high)]
            right = jnp.concatenate(right, 0)
            total = jnp.dot(left, right, preferred_element_type=F32)
            out_ref[n, t * ATOM:(t + 1) * ATOM, :] = total.astype(out_ref.dtype)

    streamed(8, fetch, wait, compute)


def mirror_kernel(tab, place, x_ref, y_ref, t_ref, out_ref, held, blocks, sem):
    co = place[0]
    for xz in range(8):
        held[pl.ds(4 * xz + 2 * co, 2)] = x_ref[xz]
        held[pl.ds(4 * xz + 2 - 2 * co, 2)] = y_ref[xz]
    held[AR] = jnp.zeros((VECS, ATOM), BF)

    def entry(n, q):
        return tab[2 * piece_at(place, n) * M_LEN + q]

    def fetch(n):
        for q in range(33):
            source = t_ref.at[lax.shift_right_logical(entry(n, q), 6)]
            pltpu.make_async_copy(source, blocks.at[n, q], sem.at[n]).start()

    def wait(n):
        pltpu.make_async_copy(t_ref.at[pl.ds(0, 33)], blocks.at[n], sem.at[n]).wait()

    def compute(n):
        for t, (low, high) in enumerate(((0, 17), (17, 33))):
            left = [held[jnp.bitwise_and(entry(n, q), 63)] for q in range(low, high)]
            left = jnp.concatenate(left, 1)
            right = jnp.concatenate([blocks[n, q] for q in range(low, high)], 0)
            total = jnp.dot(left, right, preferred_element_type=F32)
            out_ref[n, t] = total.astype(out_ref.dtype)

    streamed(8, fetch, wait, compute)


def gathered_kernel(got_ref, out_ref):
    total = got_ref[0].astype(F32)
    for i in range(1, 8):
        total = total + got_ref[i].astype(F32)
    out_ref[...] = jnp.swapaxes(total, 1, 2).reshape(2 * ATOM, VECS)


def both_kernel(mine_ref, theirs_ref, out_ref):
    out_ref[...] = (mine_ref[...] + theirs_ref[...].astype(F32)).astype(BF)


SMEM = pl.BlockSpec(memory_space=pltpu.SMEM)
VMEM = pl.BlockSpec(memory_space=pltpu.VMEM)
ANY = pl.BlockSpec(memory_space=pl.ANY)
PARAMS = pltpu.CompilerParams(vmem_limit_bytes=24 * 1024 * 1024)
PIECE = (2 * ATOM, VECS)
BLOCKS = (2, ATOM, VECS)


def like(shape, dtype):
    return jax.ShapeDtypeStruct(shape, dtype)


def call(kernel, out_shape, scalars, arrays, scratch=(), blocks=(), flops=0, size=2**20, name=None):
    single = not isinstance(out_shape, tuple)
    return pl.pallas_call(
        kernel,
        out_shape=out_shape,
        in_specs=[SMEM] * len(scalars) + [VMEM] * len(arrays) + [ANY] * len(blocks),
        out_specs=VMEM if single else (VMEM,) * len(out_shape),
        scratch_shapes=list(scratch),
        compiler_params=PARAMS,
        cost_estimate=pl.CostEstimate(flops=flops, bytes_accessed=size, transcendentals=0),
        name=name,
    )(*scalars, *arrays, *blocks)


def shift_of(column):
    r = column // 2
    return (r // 2 - r % 4 + 2 * (column % 2)) % 4


def owners(r, c):
    column = 2 * r + c // 8
    y, xl = (c % 8 // 2 + shift_of(column)) % 4, c % 2
    return (2 * y + xl) * 16 + column


TO_COL = [(r * 16 + c, owners(r, c)) for r in range(8) for c in range(16)]
TO_ROW = [(d, s) for s, d in TO_COL]
SWAP = [(0, 1), (1, 0)]


def local(vectors, widths, tiles, block_rows, block_cols, block_count):
    row = lax.axis_index(ROWS)
    col = lax.axis_index(COLS)
    place = jnp.stack([lax.axis_index("co"), shift_of(col)]).astype(jnp.int32)
    tile_set = tiles[0, 0]
    direct_tab, mirror_tab = tables(
        block_rows[0, 0], block_cols[0, 0], block_count[0, 0], row, col
    )
    work = dict(blocks=(tile_set,), flops=2 * SLOTS * ATOM**3, size=2**23)

    def direct(far, tab, col_block):
        return call(
            functools.partial(direct_kernel, far),
            like((8, *PIECE), BF if far else F32),
            (tab, place),
            (col_block,),
            [
                pltpu.VMEM((AC + 1, ATOM, VECS), BF),
                pltpu.VMEM((8, 17, ATOM, ATOM), BF),
                pltpu.SemaphoreType.DMA((8,)),
            ],
            name="direct_far" if far else "direct_own",
            **work,
        )

    def exchange(x, axes):
        return lax.all_to_all(x, axes, split_axis=0, concat_axis=0, tiled=True)

    def apply_matrix(plain, flipped):
        piece = lax.ppermute(plain, ALL, TO_COL)
        near = exchange(flipped, ("xh", "z"))
        piece, near = lax.optimization_barrier((piece, near))
        far = lax.ppermute(near, "co", SWAP)
        col_block = exchange(jnp.broadcast_to(piece[None], (8, *PIECE)), ROWS)
        mirror = call(
            mirror_kernel,
            like((8, *BLOCKS), BF),
            (mirror_tab, place),
            (near, far),
            [
                pltpu.VMEM((AR + 1, VECS, ATOM), BF),
                pltpu.VMEM((8, 33, ATOM, ATOM), BF),
                pltpu.SemaphoreType.DMA((8,)),
            ],
            name="mirror",
            **work,
        )
        col_block, mirror = lax.optimization_barrier((col_block, mirror))
        got = exchange(mirror, ROWS)
        other = direct(1, direct_tab, col_block)
        other, got = lax.optimization_barrier((other, got))
        theirs = lax.ppermute(other, "co", SWAP)
        gathered = call(gathered_kernel, like(PIECE, F32), (), (got,), name="gathered")
        back = lax.ppermute(gathered, ALL, TO_ROW)
        col_block, gathered = lax.optimization_barrier((col_block, gathered))
        mine = direct(0, direct_tab, col_block)
        both = call(both_kernel, like((8, *PIECE), BF), (), (mine, theirs), name="both")
        own = exchange(both, ("xh", "z"))
        return own, back

    forms = (like(PIECE, BF), like((8, *BLOCKS), BF))
    plain, flipped = call(first_kernel, forms, (widths,), (vectors,), name="first")
    parts = apply_matrix(plain, flipped)
    second, plain, flipped = call(
        second_kernel, (like(PIECE, F32), *forms), (widths,), (*parts, vectors), name="second"
    )
    parts = apply_matrix(plain, flipped)
    return call(
        last_kernel, like(PIECE, F32), (widths,), (*parts, vectors, second), name="last"
    )

def solution(mesh):
    split = Mesh(mesh.devices.reshape(4, 2, 2, 4, 2), ALL)
    return jax.shard_map(
        local,
        mesh=split,
        in_specs=(
            P(ALL, None),
            P(ALL),
            P(ROWS, COLS, None, None, None),
            P(ROWS, COLS, None),
            P(ROWS, COLS, None),
            P(ROWS, COLS),
        ),
        out_specs=P(ALL, None),
        check_vma=False,
    )
```

```python
import functools

import jax
import jax.numpy as jnp
from jax import lax
from jax.experimental import pallas as pl
from jax.experimental.pallas import tpu as pltpu
from jax.sharding import Mesh
from jax.sharding import PartitionSpec as P

CENTER = 0.25
ATOM = 128
VECS = 128
AR = 32
AC = 16
SLOTS = 256
N_ROW = 8
N_COL = 16
BF = jnp.bfloat16
F32 = jnp.float32
ROWS = ("y", "xl")
COLS = ("xh", "z", "co")
ALL = ROWS + COLS
D_LEN = 9
M_LEN = 17


def tables(slot_rows, slot_cols, count, row, col):
    place = jnp.where(jnp.arange(SLOTS) < count, slot_rows * AC + slot_cols, -1)

    def pack(rows, cols, index, zero):
        want = (rows * AC + cols).reshape(-1, 1)
        entry = jnp.arange(SLOTS)[None, :] * 64 + index.reshape(-1, 1) - zero
        return zero + jnp.sum(jnp.where(place[None, :] == want, entry, 0), axis=1)

    a = jnp.arange(AR)[:, None]
    q = jnp.arange(D_LEN)[None, :]
    ga = row * AR + a
    gb = col * AC + 2 * q
    odd = ga % 2 == 1
    main = 2 * q + jnp.where(odd, ga <= gb + 1, ga > gb).astype(jnp.int32)
    extra = ga - 1 - col * AC
    extra = jnp.where(odd & (extra >= 0) & (extra < AC), extra, -AC * AR)
    b = jnp.where(q < 8, main, extra)
    direct = pack(a + 0 * b, b, b, AC)

    b = jnp.arange(AC)[:, None]
    q = jnp.arange(M_LEN)[None, :]
    gb = col * AC + b
    ga = row * AR + 2 * q
    odd = gb % 2 == 1
    main = 2 * q + jnp.where(odd, ga + 1 <= gb, ga > gb).astype(jnp.int32)
    extra = gb + 1 - row * AR
    extra = jnp.where((~odd) & (extra >= 0) & (extra < AR), extra, -AR)
    a = jnp.where(q < 16, main, extra)
    mirror = pack(a, b + 0 * a, a, AR)
    return direct, mirror


def keep_of(widths, shape, axis):
    place = lax.broadcasted_iota(jnp.int32, shape, axis)
    atom = lax.broadcasted_iota(jnp.int32, shape, 0)
    return (place < jnp.where(atom == 0, widths[0], widths[1])).astype(F32)


def send_forms(current, plain_ref, flip_ref):
    plain_ref[...] = current.reshape(2 * ATOM, VECS).astype(BF)
    flipped = jnp.swapaxes(current, 1, 2).astype(BF)
    for k in range(8):
        flip_ref[k] = flipped


def first_kernel(widths, vectors_ref, plain_ref, flip_ref):
    shape = (2, ATOM, VECS)
    first = vectors_ref[...].reshape(shape) * keep_of(widths, shape, 1)
    send_forms(first, plain_ref, flip_ref)


def applied(widths, own_ref, back_ref):
    shape = (2, ATOM, VECS)
    total = back_ref[...]
    for k in range(8):
        total = total + own_ref[k].astype(F32)
    return total.reshape(shape) * keep_of(widths, shape, 1)


def second_kernel(widths, own_ref, back_ref, vectors_ref, out_ref, plain_ref, flip_ref):
    shape = (2, ATOM, VECS)
    first = vectors_ref[...].reshape(shape) * keep_of(widths, shape, 1)
    second = applied(widths, own_ref, back_ref) - CENTER * first
    out_ref[...] = second.reshape(2 * ATOM, VECS)
    send_forms(second, plain_ref, flip_ref)


def last_kernel(widths, own_ref, back_ref, vectors_ref, second_ref, out_ref):
    shape = (2, ATOM, VECS)
    first = vectors_ref[...].reshape(shape) * keep_of(widths, shape, 1)
    third = applied(widths, own_ref, back_ref)
    out = 2.0 * (third - CENTER * second_ref[...].reshape(shape)) - first
    out_ref[...] = out.reshape(2 * ATOM, VECS)


def piece_at(place, i):
    y, xl = i // 2, i % 2
    return 2 * jnp.bitwise_and(y - place[1] + 4, 3) + xl


def direct_kernel(tab, place, x_ref, t_ref, mine_ref, other_ref, held):
    co = place[0]
    for i in range(8):
        held[pl.ds(2 * piece_at(place, i), 2)] = x_ref[i].reshape(2, ATOM, VECS)
    held[AC] = jnp.zeros((ATOM, VECS), BF)

    def product(a, q, n):
        blocks, xs = [], []
        for k in range(n):
            e = tab[a * D_LEN + q + k]
            blocks.append(t_ref[lax.shift_right_logical(e, 6)])
            xs.append(held[jnp.bitwise_and(e, 63)])
        if n == 1:
            left, right = blocks[0], xs[0]
        else:
            left, right = jnp.concatenate(blocks, 1), jnp.concatenate(xs, 0)
        return jnp.dot(left, right, preferred_element_type=F32)

    def step(xz, carry):
        for which, out in ((0, mine_ref), (1, other_ref)):
            for t in range(2):
                a = 4 * xz + 2 * (co if which == 0 else 1 - co) + t
                total = product(a, 0, 8)
                if t:
                    total = total + product(a, 8, 1)
                out[xz, t * ATOM:(t + 1) * ATOM, :] = total.astype(out.dtype)
        return carry

    lax.fori_loop(0, 8, step, 0, unroll=True)


def mirror_kernel(tab, place, x_ref, y_ref, t_ref, out_ref, held):
    co = place[0]
    for xz in range(8):
        held[pl.ds(4 * xz + 2 * co, 2)] = x_ref[xz]
        held[pl.ds(4 * xz + 2 - 2 * co, 2)] = y_ref[xz]
    held[AR] = jnp.zeros((VECS, ATOM), BF)

    def product(b, q, n):
        blocks, xs = [], []
        for k in range(n):
            e = tab[b * M_LEN + q + k]
            blocks.append(t_ref[lax.shift_right_logical(e, 6)])
            xs.append(held[jnp.bitwise_and(e, 63)])
        if n == 1:
            left, right = xs[0], blocks[0]
        else:
            left, right = jnp.concatenate(xs, 1), jnp.concatenate(blocks, 0)
        return jnp.dot(left, right, preferred_element_type=F32)

    def step(i, carry):
        k = piece_at(place, i)
        for t in range(2):
            b = 2 * k + t
            total = product(b, 0, 8) + product(b, 8, 8)
            if not t:
                total = total + product(b, 16, 1)
            out_ref[i, t] = total.astype(out_ref.dtype)
        return carry

    lax.fori_loop(0, 8, step, 0, unroll=True)


def gathered_kernel(got_ref, out_ref):
    total = got_ref[0].astype(F32)
    for i in range(1, 8):
        total = total + got_ref[i].astype(F32)
    out_ref[...] = total.astype(out_ref.dtype)


def turned_kernel(sum_ref, out_ref):
    out_ref[...] = jnp.swapaxes(sum_ref[...].astype(F32), 1, 2).reshape(2 * ATOM, VECS)


def both_kernel(mine_ref, theirs_ref, out_ref):
    out_ref[...] = (mine_ref[...] + theirs_ref[...].astype(F32)).astype(BF)


SMEM = pl.BlockSpec(memory_space=pltpu.SMEM)
VMEM = pl.BlockSpec(memory_space=pltpu.VMEM)
PARAMS = pltpu.CompilerParams(vmem_limit_bytes=24 * 1024 * 1024)
PIECE = (2 * ATOM, VECS)
BLOCKS = (2, ATOM, VECS)


def like(shape, dtype):
    return jax.ShapeDtypeStruct(shape, dtype)


def call(kernel, out_shape, scalars, arrays, scratch=(), flops=0, size=2**20, name=None):
    single = not isinstance(out_shape, tuple)
    return pl.pallas_call(
        kernel,
        out_shape=out_shape,
        in_specs=[SMEM] * len(scalars) + [VMEM] * len(arrays),
        out_specs=VMEM if single else (VMEM,) * len(out_shape),
        scratch_shapes=list(scratch),
        compiler_params=PARAMS,
        cost_estimate=pl.CostEstimate(flops=flops, bytes_accessed=size, transcendentals=0),
        name=name,
    )(*scalars, *arrays)


def shift_of(column):
    r = column // 2
    return (r // 2 - r % 4 + 2 * (column % 2)) % 4


def owners(r, c):
    column = 2 * r + c // 8
    y, xl = (c % 8 // 2 + shift_of(column)) % 4, c % 2
    return (2 * y + xl) * 16 + column


TO_COL = [(r * 16 + c, owners(r, c)) for r in range(8) for c in range(16)]
TO_ROW = [(d, s) for s, d in TO_COL]
SWAP = [(0, 1), (1, 0)]


def local(vectors, widths, tiles, block_rows, block_cols, block_count):
    row = lax.axis_index(ROWS)
    col = lax.axis_index(COLS)
    place = jnp.stack([lax.axis_index("co"), shift_of(col)]).astype(jnp.int32)
    tile_set = tiles[0, 0]
    direct_tab, mirror_tab = tables(
        block_rows[0, 0], block_cols[0, 0], block_count[0, 0], row, col
    )
    work = dict(flops=2 * SLOTS * ATOM**3, size=2**23)

    def exchange(x, axes):
        return lax.all_to_all(x, axes, split_axis=0, concat_axis=0, tiled=True)

    def apply_matrix(plain, flipped, sent):
        piece = lax.ppermute(plain, ALL, TO_COL)
        near = exchange(flipped, ("xh", "z"))
        piece, near = lax.optimization_barrier((piece, near))
        far = lax.ppermute(near, "co", SWAP)
        col_block = exchange(jnp.broadcast_to(piece[None], (8, *PIECE)), ROWS)
        mirror = call(
            mirror_kernel,
            like((8, *BLOCKS), BF),
            (mirror_tab, place),
            (near, far, tile_set),
            [pltpu.VMEM((AR + 1, VECS, ATOM), BF)],
            name="mirror",
            **work,
        )
        col_block, mirror = lax.optimization_barrier((col_block, mirror))
        got = exchange(mirror, ROWS)
        mine, other = call(
            direct_kernel,
            (like((8, *PIECE), F32), like((8, *PIECE), BF)),
            (direct_tab, place),
            (col_block, tile_set),
            [pltpu.VMEM((AC + 1, ATOM, VECS), BF)],
            name="direct",
            **work,
        )
        other, got = lax.optimization_barrier((other, got))
        theirs = lax.ppermute(other, "co", SWAP)
        both = call(both_kernel, like((8, *PIECE), BF), (), (mine, theirs), name="both")
        own = exchange(both, ("xh", "z"))
        gathered = call(gathered_kernel, like(BLOCKS, sent), (), (got,), name="gathered")
        back = lax.ppermute(gathered, ALL, TO_ROW)
        turned = call(turned_kernel, like(PIECE, F32), (), (back,), name="turned")
        return own, turned

    forms = (like(PIECE, BF), like((8, *BLOCKS), BF))
    plain, flipped = call(first_kernel, forms, (widths,), (vectors,), name="first")
    parts = apply_matrix(plain, flipped, F32)
    second, plain, flipped = call(
        second_kernel, (like(PIECE, F32), *forms), (widths,), (*parts, vectors), name="second"
    )
    parts = apply_matrix(plain, flipped, BF)
    return call(
        last_kernel, like(PIECE, F32), (widths,), (*parts, vectors, second), name="last"
    )

def solution(mesh):
    split = Mesh(mesh.devices.reshape(4, 2, 2, 4, 2), ALL)
    return jax.shard_map(
        local,
        mesh=split,
        in_specs=(
            P(ALL, None),
            P(ALL),
            P(ROWS, COLS, None, None, None),
            P(ROWS, COLS, None),
            P(ROWS, COLS, None),
            P(ROWS, COLS),
        ),
        out_specs=P(ALL, None),
        check_vma=False,
    )
```

```python
import functools

import jax
import jax.numpy as jnp
from jax import lax
from jax.experimental import pallas as pl
from jax.experimental.pallas import tpu as pltpu
from jax.sharding import Mesh
from jax.sharding import PartitionSpec as P

CENTER = 0.25
ATOM = 128
VECS = 128
AR = 32
AC = 16
SLOTS = 256
N_ROW = 8
N_COL = 16
BF = jnp.bfloat16
F32 = jnp.float32
ROWS = ("y", "xl")
COLS = ("xh", "z", "co")
ALL = ROWS + COLS
D_LEN = 9
M_LEN = 17
PIECE = (2 * ATOM, VECS)
BLOCKS = (2, ATOM, VECS)


def tables(slot_rows, slot_cols, count, row, col):
    place = jnp.where(jnp.arange(SLOTS) < count, slot_rows * AC + slot_cols, -1)

    def pack(rows, cols, index, zero):
        want = (rows * AC + cols).reshape(-1, 1)
        entry = jnp.arange(SLOTS)[None, :] * 64 + index.reshape(-1, 1) - zero
        return zero + jnp.sum(jnp.where(place[None, :] == want, entry, 0), axis=1)

    a = jnp.arange(AR)[:, None]
    q = jnp.arange(D_LEN)[None, :]
    ga = row * AR + a
    gb = col * AC + 2 * q
    odd = ga % 2 == 1
    main = 2 * q + jnp.where(odd, ga <= gb + 1, ga > gb).astype(jnp.int32)
    extra = ga - 1 - col * AC
    extra = jnp.where(odd & (extra >= 0) & (extra < AC), extra, -AC * AR)
    b = jnp.where(q < 8, main, extra)
    direct = pack(a + 0 * b, b, b, AC)

    b = jnp.arange(AC)[:, None]
    q = jnp.arange(M_LEN)[None, :]
    gb = col * AC + b
    ga = row * AR + 2 * q
    odd = gb % 2 == 1
    main = 2 * q + jnp.where(odd, ga + 1 <= gb, ga > gb).astype(jnp.int32)
    extra = gb + 1 - row * AR
    extra = jnp.where((~odd) & (extra >= 0) & (extra < AR), extra, -AR)
    a = jnp.where(q < 16, main, extra)
    mirror = pack(a, b + 0 * a, a, AR)
    return direct, mirror


def keep_of(widths, shape, axis):
    place = lax.broadcasted_iota(jnp.int32, shape, axis)
    atom = lax.broadcasted_iota(jnp.int32, shape, 0)
    return (place < jnp.where(atom == 0, widths[0], widths[1])).astype(F32)


def flip(current):
    return jnp.swapaxes(current, 1, 2)


def first_kernel(widths, vectors_ref, plain_ref, flip_ref):
    first = vectors_ref[...].reshape(BLOCKS) * keep_of(widths, BLOCKS, 1)
    plain_ref[...] = first.reshape(PIECE).astype(BF)
    flip_ref[...] = flip(first).astype(BF)


def own_sum(own_ref):
    total = own_ref[0].astype(F32)
    for k in range(1, 8):
        total = total + own_ref[k].astype(F32)
    return total.reshape(BLOCKS)


def second_part_kernel(widths, own_ref, vectors_ref, out_ref):
    keep = keep_of(widths, BLOCKS, 1)
    part = own_sum(own_ref) * keep - CENTER * (vectors_ref[...].reshape(BLOCKS) * keep)
    out_ref[...] = part.reshape(PIECE)


def second_col_kernel(widths, got_ref, part_ref, back_ref, copies_ref):
    total = got_ref[0].astype(F32)
    for i in range(1, 8):
        total = total + got_ref[i].astype(F32)
    total = flip(total)
    back_ref[...] = total.reshape(PIECE)
    second = total * keep_of(widths, BLOCKS, 1) + part_ref[...].reshape(BLOCKS)
    second = second.reshape(PIECE).astype(BF)
    for i in range(8):
        copies_ref[i] = second


def second_row_kernel(widths, back_ref, part_ref, out_ref, flip_ref):
    second = back_ref[...].reshape(BLOCKS) * keep_of(widths, BLOCKS, 1)
    second = second + part_ref[...].reshape(BLOCKS)
    out_ref[...] = second.reshape(PIECE)
    flip_ref[...] = flip(second).astype(BF)


def last_part_kernel(widths, own_ref, vectors_ref, second_ref, out_ref):
    keep = keep_of(widths, BLOCKS, 1)
    first = vectors_ref[...].reshape(BLOCKS) * keep
    third = own_sum(own_ref) * keep
    part = 2.0 * (third - CENTER * second_ref[...].reshape(BLOCKS)) - first
    out_ref[...] = part.reshape(PIECE)


def gathered_kernel(got_ref, out_ref):
    total = got_ref[0].astype(F32)
    for i in range(1, 8):
        total = total + got_ref[i].astype(F32)
    out_ref[...] = flip(total).reshape(PIECE).astype(out_ref.dtype)


def last_kernel(widths, back_ref, part_ref, out_ref):
    back = back_ref[...].astype(F32).reshape(BLOCKS) * keep_of(widths, BLOCKS, 1)
    out_ref[...] = part_ref[...] + 2.0 * back.reshape(PIECE)


def piece_at(place, i):
    y, xl = i // 2, i % 2
    return 2 * jnp.bitwise_and(y - place[1] + 4, 3) + xl


def direct_kernel(tab, place, x_ref, t_ref, mine_ref, other_ref, held):
    co = place[0]
    for i in range(8):
        held[pl.ds(2 * piece_at(place, i), 2)] = x_ref[i].reshape(2, ATOM, VECS)
    held[AC] = jnp.zeros((ATOM, VECS), BF)

    def product(a, q, n):
        blocks, xs = [], []
        for k in range(n):
            e = tab[a * D_LEN + q + k]
            blocks.append(t_ref[lax.shift_right_logical(e, 6)])
            xs.append(held[jnp.bitwise_and(e, 63)])
        if n == 1:
            left, right = blocks[0], xs[0]
        else:
            left, right = jnp.concatenate(blocks, 1), jnp.concatenate(xs, 0)
        return jnp.dot(left, right, preferred_element_type=F32)

    def step(xz, carry):
        for which, out in ((0, mine_ref), (1, other_ref)):
            for t in range(2):
                a = 4 * xz + 2 * (co if which == 0 else 1 - co) + t
                total = product(a, 0, 8)
                if t:
                    total = total + product(a, 8, 1)
                out[xz, t * ATOM:(t + 1) * ATOM, :] = total.astype(out.dtype)
        return carry

    lax.fori_loop(0, 8, step, 0, unroll=True)


def mirror_kernel(tab, place, z0_ref, z1_ref, z2_ref, z3_ref, c0_ref, c1_ref, c2_ref, c3_ref,
                  t_ref, out_ref, held):
    co, z, xh = place[0], place[2], place[3]
    for core, refs in (
        (co, (z0_ref, z1_ref, z2_ref, z3_ref)),
        (1 - co, (c0_ref, c1_ref, c2_ref, c3_ref)),
    ):
        for s, ref in enumerate(refs):
            for rel in range(2):
                c = 8 * jnp.bitwise_xor(xh, rel) + 2 * jnp.bitwise_and(z - s + 4, 3) + core
                held[pl.ds(2 * c, 2)] = ref[rel]
    held[AR] = jnp.zeros((VECS, ATOM), BF)

    def product(b, q, n):
        blocks, xs = [], []
        for k in range(n):
            e = tab[b * M_LEN + q + k]
            blocks.append(t_ref[lax.shift_right_logical(e, 6)])
            xs.append(held[jnp.bitwise_and(e, 63)])
        if n == 1:
            left, right = xs[0], blocks[0]
        else:
            left, right = jnp.concatenate(xs, 1), jnp.concatenate(blocks, 0)
        return jnp.dot(left, right, preferred_element_type=F32)

    def step(i, carry):
        k = piece_at(place, i)
        for t in range(2):
            b = 2 * k + t
            total = product(b, 0, 8) + product(b, 8, 8)
            if not t:
                total = total + product(b, 16, 1)
            out_ref[i, t] = total.astype(out_ref.dtype)
        return carry

    lax.fori_loop(0, 8, step, 0, unroll=True)


def both_kernel(mine_ref, theirs_ref, out_ref):
    out_ref[...] = (mine_ref[...] + theirs_ref[...].astype(F32)).astype(BF)


SMEM = pl.BlockSpec(memory_space=pltpu.SMEM)
VMEM = pl.BlockSpec(memory_space=pltpu.VMEM)
PARAMS = pltpu.CompilerParams(vmem_limit_bytes=24 * 1024 * 1024)
def like(shape, dtype):
    return jax.ShapeDtypeStruct(shape, dtype)


def call(kernel, out_shape, scalars, arrays, scratch=(), flops=0, size=2**20, name=None):
    single = not isinstance(out_shape, tuple)
    return pl.pallas_call(
        kernel,
        out_shape=out_shape,
        in_specs=[SMEM] * len(scalars) + [VMEM] * len(arrays),
        out_specs=VMEM if single else (VMEM,) * len(out_shape),
        scratch_shapes=list(scratch),
        compiler_params=PARAMS,
        cost_estimate=pl.CostEstimate(flops=flops, bytes_accessed=size, transcendentals=0),
        name=name,
    )(*scalars, *arrays)


def shift_of(column):
    r = column // 2
    return (r // 2 - r % 4 + 2 * (column % 2)) % 4


def owners(r, c):
    column = 2 * r + c // 8
    y, xl = (c % 8 // 2 + shift_of(column)) % 4, c % 2
    return (2 * y + xl) * 16 + column


TO_COL = [(r * 16 + c, owners(r, c)) for r in range(8) for c in range(16)]
TO_ROW = [(d, s) for s, d in TO_COL]
SWAP = [(0, 1), (1, 0)]


def turn(s):
    return [(k, (k + s) % 4) for k in range(4)]


def local(vectors, widths, tiles, block_rows, block_cols, block_count):
    row = lax.axis_index(ROWS)
    col = lax.axis_index(COLS)
    place = jnp.stack(
        [lax.axis_index("co"), shift_of(col), lax.axis_index("z"), lax.axis_index("xh")]
    ).astype(jnp.int32)
    tile_set = tiles[0, 0]
    direct_tab, mirror_tab = tables(
        block_rows[0, 0], block_cols[0, 0], block_count[0, 0], row, col
    )
    work = dict(flops=2 * SLOTS * ATOM**3, size=2**23)

    def exchange(x, axes):
        return lax.all_to_all(x, axes, split_axis=0, concat_axis=0, tiled=True)

    def row_block(flipped):
        far = lax.ppermute(flipped, "xh", SWAP)
        pair = jnp.stack([flipped, far])
        turned = [pair] + [lax.ppermute(pair, "z", turn(s)) for s in (1, 2, 3)]
        return (*turned, *(lax.ppermute(t, "co", SWAP) for t in turned))

    def products(col_block, flipped):
        mine, other = call(
            direct_kernel,
            (like((8, *PIECE), F32), like((8, *PIECE), BF)),
            (direct_tab, place),
            (col_block, tile_set),
            [pltpu.VMEM((AC + 1, ATOM, VECS), BF)],
            name="direct",
            **work,
        )
        theirs = lax.ppermute(other, "co", SWAP)
        both = call(both_kernel, like((8, *PIECE), BF), (), (mine, theirs), name="both")
        own = exchange(both, ("xh", "z"))
        mirror = call(
            mirror_kernel,
            like((8, *BLOCKS), BF),
            (mirror_tab, place),
            (*row_block(flipped), tile_set),
            [pltpu.VMEM((AR + 1, VECS, ATOM), BF)],
            name="mirror",
            **work,
        )
        own, mirror = lax.optimization_barrier((own, mirror))
        return own, exchange(mirror, ROWS)

    plain, flipped = call(
        first_kernel, (like(PIECE, BF), like(BLOCKS, BF)), (widths,), (vectors,), name="first"
    )
    piece = lax.ppermute(plain, ALL, TO_COL)
    col_widths = lax.ppermute(
        jnp.broadcast_to(widths.astype(F32)[:, None], (2, VECS)), ALL, TO_COL
    )[:, 0].astype(jnp.int32)
    col_block = exchange(jnp.broadcast_to(piece[None], (8, *PIECE)), ROWS)
    own, got = products(col_block, flipped)
    part = call(second_part_kernel, like(PIECE, F32), (widths,), (own, vectors), name="part")
    col_part = lax.ppermute(part, ALL, TO_COL)
    back, copies = call(
        second_col_kernel,
        (like(PIECE, F32), like((8, *PIECE), BF)),
        (col_widths,),
        (got, col_part),
        name="second_col",
    )
    back = lax.ppermute(back, ALL, TO_ROW)
    col_block = exchange(copies, ROWS)
    second, flipped = call(
        second_row_kernel,
        (like(PIECE, F32), like(BLOCKS, BF)),
        (widths,),
        (back, part),
        name="second_row",
    )
    own, got = products(col_block, flipped)
    part = call(
        last_part_kernel, like(PIECE, F32), (widths,), (own, vectors, second), name="last_part"
    )
    back = call(gathered_kernel, like(PIECE, BF), (), (got,), name="gathered")
    back = lax.ppermute(back, ALL, TO_ROW)
    return call(last_kernel, like(PIECE, F32), (widths,), (back, part), name="last")


def solution(mesh):
    split = Mesh(mesh.devices.reshape(4, 2, 2, 4, 2), ALL)
    return jax.shard_map(
        local,
        mesh=split,
        in_specs=(
            P(ALL, None),
            P(ALL),
            P(ROWS, COLS, None, None, None),
            P(ROWS, COLS, None),
            P(ROWS, COLS, None),
            P(ROWS, COLS),
        ),
        out_specs=P(ALL, None),
        check_vma=False,
    )
```

```python
import functools

import jax
import jax.numpy as jnp
from jax import lax
from jax.experimental import pallas as pl
from jax.experimental.pallas import tpu as pltpu
from jax.sharding import Mesh
from jax.sharding import PartitionSpec as P

CENTER = 0.25
ATOM = 128
VECS = 128
AR = 32
AC = 16
SLOTS = 256
N_ROW = 8
N_COL = 16
BF = jnp.bfloat16
F32 = jnp.float32
ROWS = ("y", "xl")
COLS = ("xh", "z", "co")
ALL = ROWS + COLS
D_LEN = 9
M_LEN = 17
PIECE = (2 * ATOM, VECS)
BLOCKS = (2, ATOM, VECS)


def tables(slot_rows, slot_cols, count, row, col):
    place = jnp.where(jnp.arange(SLOTS) < count, slot_rows * AC + slot_cols, -1)

    def pack(rows, cols, index, zero):
        want = (rows * AC + cols).reshape(-1, 1)
        entry = jnp.arange(SLOTS)[None, :] * 64 + index.reshape(-1, 1) - zero
        return zero + jnp.sum(jnp.where(place[None, :] == want, entry, 0), axis=1)

    a = jnp.arange(AR)[:, None]
    q = jnp.arange(D_LEN)[None, :]
    ga = row * AR + a
    gb = col * AC + 2 * q
    odd = ga % 2 == 1
    main = 2 * q + jnp.where(odd, ga <= gb + 1, ga > gb).astype(jnp.int32)
    extra = ga - 1 - col * AC
    extra = jnp.where(odd & (extra >= 0) & (extra < AC), extra, -AC * AR)
    b = jnp.where(q < 8, main, extra)
    direct = pack(a + 0 * b, b, b, AC)

    b = jnp.arange(AC)[:, None]
    q = jnp.arange(M_LEN)[None, :]
    gb = col * AC + b
    ga = row * AR + 2 * q
    odd = gb % 2 == 1
    main = 2 * q + jnp.where(odd, ga + 1 <= gb, ga > gb).astype(jnp.int32)
    extra = gb + 1 - row * AR
    extra = jnp.where((~odd) & (extra >= 0) & (extra < AR), extra, -AR)
    a = jnp.where(q < 16, main, extra)
    mirror = pack(a, b + 0 * a, a, AR)
    return direct, mirror


def keep_of(widths, shape, axis):
    place = lax.broadcasted_iota(jnp.int32, shape, axis)
    atom = lax.broadcasted_iota(jnp.int32, shape, 0)
    return (place < jnp.where(atom == 0, widths[0], widths[1])).astype(F32)


def flip(current):
    return jnp.swapaxes(current, 1, 2)


def first_kernel(widths, vectors_ref, plain_ref, flip_ref):
    first = vectors_ref[...].reshape(BLOCKS) * keep_of(widths, BLOCKS, 1)
    plain_ref[: 2 * ATOM] = first.reshape(PIECE).astype(BF)
    atom = lax.broadcasted_iota(jnp.int32, (16, VECS), 0) // 8
    width = jnp.where(atom == 0, widths[0], widths[1])
    plain_ref[2 * ATOM:] = width.astype(F32).astype(BF)
    flip_ref[...] = flip(first).astype(BF)


def own_sum(own_ref):
    total = own_ref[0].astype(F32)
    for k in range(1, 8):
        total = total + own_ref[k].astype(F32)
    return total.reshape(BLOCKS)


def second_part_kernel(widths, own_ref, vectors_ref, out_ref):
    keep = keep_of(widths, BLOCKS, 1)
    part = own_sum(own_ref) * keep - CENTER * (vectors_ref[...].reshape(BLOCKS) * keep)
    out_ref[...] = part.reshape(PIECE)


def second_col_kernel(got_ref, part_ref, widths_ref, back_ref, copies_ref):
    total = got_ref[0].astype(F32)
    for i in range(1, 8):
        total = total + got_ref[i].astype(F32)
    total = flip(total)
    back_ref[...] = total.reshape(PIECE)
    place = lax.broadcasted_iota(jnp.int32, (ATOM, VECS), 0).astype(F32)
    for atom in range(2):
        width = widths_ref[pl.ds(2 * ATOM, 16)].astype(F32)[8 * atom:8 * atom + 1]
        keep = (place < width).astype(F32)
        rows = pl.ds(atom * ATOM, ATOM)
        second = (total[atom] * keep + part_ref[rows]).astype(BF)
        for i in range(8):
            copies_ref[i, rows] = second


def second_row_kernel(widths, back_ref, part_ref, out_ref, flip_ref):
    second = back_ref[...].reshape(BLOCKS) * keep_of(widths, BLOCKS, 1)
    second = second + part_ref[...].reshape(BLOCKS)
    out_ref[...] = second.reshape(PIECE)
    flip_ref[...] = flip(second).astype(BF)


def last_part_kernel(widths, own_ref, vectors_ref, second_ref, out_ref):
    keep = keep_of(widths, BLOCKS, 1)
    first = vectors_ref[...].reshape(BLOCKS) * keep
    third = own_sum(own_ref) * keep
    part = 2.0 * (third - CENTER * second_ref[...].reshape(BLOCKS)) - first
    out_ref[...] = part.reshape(PIECE)


def gathered_kernel(got_ref, out_ref):
    total = got_ref[0].astype(F32)
    for i in range(1, 8):
        total = total + got_ref[i].astype(F32)
    out_ref[...] = flip(total).reshape(PIECE).astype(out_ref.dtype)


def last_kernel(widths, back_ref, part_ref, out_ref):
    back = back_ref[...].astype(F32).reshape(BLOCKS) * keep_of(widths, BLOCKS, 1)
    out_ref[...] = part_ref[...] + 2.0 * back.reshape(PIECE)


def piece_at(place, i):
    y, xl = i // 2, i % 2
    return 2 * jnp.bitwise_and(y - place[1] + 4, 3) + xl


def direct_kernel(tab, place, x_ref, t_ref, mine_ref, other_ref, held):
    co = place[0]
    for i in range(8):
        held[pl.ds(2 * piece_at(place, i), 2)] = x_ref[i].reshape(2, ATOM, VECS)
    held[AC] = jnp.zeros((ATOM, VECS), BF)

    def product(a, q, n):
        blocks, xs = [], []
        for k in range(n):
            e = tab[a * D_LEN + q + k]
            blocks.append(t_ref[lax.shift_right_logical(e, 6)])
            xs.append(held[jnp.bitwise_and(e, 63)])
        if n == 1:
            left, right = blocks[0], xs[0]
        else:
            left, right = jnp.concatenate(blocks, 1), jnp.concatenate(xs, 0)
        return jnp.dot(left, right, preferred_element_type=F32)

    def step(xz, carry):
        for which, out in ((0, mine_ref), (1, other_ref)):
            for t in range(2):
                a = 4 * xz + 2 * (co if which == 0 else 1 - co) + t
                total = product(a, 0, 8)
                if t:
                    total = total + product(a, 8, 1)
                out[xz, t * ATOM:(t + 1) * ATOM, :] = total.astype(out.dtype)
        return carry

    lax.fori_loop(0, 8, step, 0, unroll=True)


def mirror_kernel(tab, place, z0_ref, z1_ref, z2_ref, z3_ref, c0_ref, c1_ref, c2_ref, c3_ref,
                  t_ref, out_ref, held):
    co, z, xh = place[0], place[2], place[3]
    for core, refs in (
        (co, (z0_ref, z1_ref, z2_ref, z3_ref)),
        (1 - co, (c0_ref, c1_ref, c2_ref, c3_ref)),
    ):
        for s, ref in enumerate(refs):
            for rel in range(2):
                c = 8 * jnp.bitwise_xor(xh, rel) + 2 * jnp.bitwise_and(z - s + 4, 3) + core
                held[pl.ds(2 * c, 2)] = ref[rel]
    held[AR] = jnp.zeros((VECS, ATOM), BF)

    def product(b, q, n):
        blocks, xs = [], []
        for k in range(n):
            e = tab[b * M_LEN + q + k]
            blocks.append(t_ref[lax.shift_right_logical(e, 6)])
            xs.append(held[jnp.bitwise_and(e, 63)])
        if n == 1:
            left, right = xs[0], blocks[0]
        else:
            left, right = jnp.concatenate(xs, 1), jnp.concatenate(blocks, 0)
        return jnp.dot(left, right, preferred_element_type=F32)

    def step(i, carry):
        k = piece_at(place, i)
        for t in range(2):
            b = 2 * k + t
            total = product(b, 0, 8) + product(b, 8, 8)
            if not t:
                total = total + product(b, 16, 1)
            out_ref[i, t] = total.astype(out_ref.dtype)
        return carry

    lax.fori_loop(0, 8, step, 0, unroll=True)


def both_kernel(mine_ref, theirs_ref, out_ref):
    out_ref[...] = (mine_ref[...] + theirs_ref[...].astype(F32)).astype(BF)


SMEM = pl.BlockSpec(memory_space=pltpu.SMEM)
VMEM = pl.BlockSpec(memory_space=pltpu.VMEM)
PARAMS = pltpu.CompilerParams(vmem_limit_bytes=24 * 1024 * 1024)
def like(shape, dtype):
    return jax.ShapeDtypeStruct(shape, dtype)


def call(kernel, out_shape, scalars, arrays, scratch=(), flops=0, size=2**20, name=None):
    single = not isinstance(out_shape, tuple)
    return pl.pallas_call(
        kernel,
        out_shape=out_shape,
        in_specs=[SMEM] * len(scalars) + [VMEM] * len(arrays),
        out_specs=VMEM if single else (VMEM,) * len(out_shape),
        scratch_shapes=list(scratch),
        compiler_params=PARAMS,
        cost_estimate=pl.CostEstimate(flops=flops, bytes_accessed=size, transcendentals=0),
        name=name,
    )(*scalars, *arrays)


def shift_of(column):
    r = column // 2
    return (r // 2 - r % 4 + 2 * (column % 2)) % 4


def owners(r, c):
    column = 2 * r + c // 8
    y, xl = (c % 8 // 2 + shift_of(column)) % 4, c % 2
    return (2 * y + xl) * 16 + column


TO_COL = [(r * 16 + c, owners(r, c)) for r in range(8) for c in range(16)]
TO_ROW = [(d, s) for s, d in TO_COL]
SWAP = [(0, 1), (1, 0)]


def turn(s):
    return [(k, (k + s) % 4) for k in range(4)]


def local(vectors, widths, tiles, block_rows, block_cols, block_count):
    row = lax.axis_index(ROWS)
    col = lax.axis_index(COLS)
    place = jnp.stack(
        [lax.axis_index("co"), shift_of(col), lax.axis_index("z"), lax.axis_index("xh")]
    ).astype(jnp.int32)
    tile_set = tiles[0, 0]
    direct_tab, mirror_tab = tables(
        block_rows[0, 0], block_cols[0, 0], block_count[0, 0], row, col
    )
    work = dict(flops=2 * SLOTS * ATOM**3, size=2**23)

    def exchange(x, axes):
        return lax.all_to_all(x, axes, split_axis=0, concat_axis=0, tiled=True)

    def row_block(flipped):
        far = lax.ppermute(flipped, "xh", SWAP)
        pair = jnp.stack([flipped, far])
        return [pair] + [lax.ppermute(pair, "z", turn(s)) for s in (1, 2, 3)]

    def products(col_block, turned):
        crossed = [lax.ppermute(t, "co", SWAP) for t in turned]
        mine, other = call(
            direct_kernel,
            (like((8, *PIECE), F32), like((8, *PIECE), BF)),
            (direct_tab, place),
            (col_block, tile_set),
            [pltpu.VMEM((AC + 1, ATOM, VECS), BF)],
            name="direct",
            **work,
        )
        theirs = lax.ppermute(other, "co", SWAP)
        both = call(both_kernel, like((8, *PIECE), BF), (), (mine, theirs), name="both")
        own = exchange(both, ("xh", "z"))
        mirror = call(
            mirror_kernel,
            like((8, *BLOCKS), BF),
            (mirror_tab, place),
            (*turned, *crossed, tile_set),
            [pltpu.VMEM((AR + 1, VECS, ATOM), BF)],
            name="mirror",
            **work,
        )
        own, mirror = lax.optimization_barrier((own, mirror))
        return own, exchange(mirror, ROWS)

    plain, flipped = call(
        first_kernel,
        (like((2 * ATOM + 16, VECS), BF), like(BLOCKS, BF)),
        (widths,),
        (vectors,),
        name="first",
    )
    piece = lax.ppermute(plain, ALL, TO_COL)
    turned, col_block = row_block(flipped), exchange(
        jnp.broadcast_to(piece[None, : 2 * ATOM], (8, *PIECE)), ROWS
    )
    turned, col_block = lax.optimization_barrier((turned, col_block))
    own, got = products(col_block, turned)
    part = call(second_part_kernel, like(PIECE, F32), (widths,), (own, vectors), name="part")
    col_part = lax.ppermute(part, ALL, TO_COL)
    back, copies = call(
        second_col_kernel,
        (like(PIECE, F32), like((8, *PIECE), BF)),
        (),
        (got, col_part, piece),
        name="second_col",
    )
    back = lax.ppermute(back, ALL, TO_ROW)
    col_block = exchange(copies, ROWS)
    second, flipped = call(
        second_row_kernel,
        (like(PIECE, F32), like(BLOCKS, BF)),
        (widths,),
        (back, part),
        name="second_row",
    )
    col_block, flipped = lax.optimization_barrier((col_block, flipped))
    own, got = products(col_block, row_block(flipped))
    part = call(
        last_part_kernel, like(PIECE, F32), (widths,), (own, vectors, second), name="last_part"
    )
    back = call(gathered_kernel, like(PIECE, BF), (), (got,), name="gathered")
    back = lax.ppermute(back, ALL, TO_ROW)
    return call(last_kernel, like(PIECE, F32), (widths,), (back, part), name="last")


def solution(mesh):
    split = Mesh(mesh.devices.reshape(4, 2, 2, 4, 2), ALL)
    return jax.shard_map(
        local,
        mesh=split,
        in_specs=(
            P(ALL, None),
            P(ALL),
            P(ROWS, COLS, None, None, None),
            P(ROWS, COLS, None),
            P(ROWS, COLS, None),
            P(ROWS, COLS),
        ),
        out_specs=P(ALL, None),
        check_vma=False,
    )
```

```python
import functools

import jax
import jax.numpy as jnp
from jax import lax
from jax.experimental import pallas as pl
from jax.experimental.pallas import tpu as pltpu
from jax.sharding import Mesh
from jax.sharding import PartitionSpec as P

CENTER = 0.25
ATOM = 128
VECS = 128
AR = 32
AC = 16
SLOTS = 256
N_ROW = 8
N_COL = 16
BF = jnp.bfloat16
F32 = jnp.float32
ROWS = ("y", "xl")
COLS = ("xh", "z", "co")
ALL = ROWS + COLS
D_LEN = 10
M_LEN = 18


def row_lists(row, col):
    t = jnp.arange(2)[None, :, None]
    q = jnp.arange(D_LEN)[None, None, :]
    ga = row * AR + 4 * jnp.arange(8)[:, None, None] + t
    m = jnp.minimum(q, 7)
    gb = col * AC + 2 * m
    main = 2 * m + jnp.where(t == 1, ga <= gb + 1, ga > gb).astype(jnp.int32)
    near = ga - t - col * AC + jnp.where(t == 1, 0, 1)
    extra = jnp.where(q == 8, near, jnp.where(t == 1, near + 2, -1))
    extra = jnp.where((extra >= 0) & (extra < AC), extra, -1)
    return jnp.where(q < 8, main, extra)


def col_lists(row, col):
    t = jnp.arange(2)[None, :, None]
    q = jnp.arange(M_LEN)[None, None, :]
    gb = col * AC + 4 * jnp.arange(4)[:, None, None] + t
    m = jnp.minimum(q, 15)
    ga = row * AR + 2 * m
    main = 2 * m + jnp.where(t == 1, ga + 1 <= gb + 2, ga > gb + 2).astype(jnp.int32)
    near = gb + 1 - row * AR
    extra = jnp.where(q == 16, near, jnp.where(t == 0, near + 2, -1))
    extra = jnp.where((extra >= 0) & (extra < AR), extra, -1)
    return jnp.where(q < 16, main, extra)


def tables(slot_rows, slot_cols, count, row, col):
    place = jnp.where(jnp.arange(SLOTS) < count, slot_rows * AC + slot_cols, -AC * AR)

    def slots(rows, cols, index):
        want = jnp.where(index < 0, -1, rows * AC + cols).reshape(-1, 1)
        entry = jnp.arange(SLOTS)[None, :] + 1
        return jnp.sum(jnp.where(place[None, :] == want, entry, 0), axis=1) - 1

    b = row_lists(row, col)[:, None]
    a = jnp.arange(AR).reshape(8, 2, 2, 1)
    direct = slots(a + 0 * b, b + 0 * a, b + 0 * a)
    a = col_lists(row, col)[:, None]
    c = jnp.arange(AC).reshape(4, 2, 2, 1)
    mirror = slots(a + 0 * c, c + 0 * a, a + 0 * c)
    lists = [jnp.maximum(x, 0).reshape(-1) for x in (b, a)]
    return lists[0], direct, lists[1], mirror


def keep_of(widths, shape, axis):
    place = lax.broadcasted_iota(jnp.int32, shape, axis)
    atom = lax.broadcasted_iota(jnp.int32, shape, 0)
    return (place < jnp.where(atom == 0, widths[0], widths[1])).astype(F32)


def send_forms(current, plain_ref, flip_ref):
    plain_ref[...] = current.reshape(2 * ATOM, VECS).astype(BF)
    flipped = jnp.swapaxes(current, 1, 2).astype(BF)
    for k in range(8):
        flip_ref[k] = flipped


def first_kernel(widths, vectors_ref, plain_ref, flip_ref):
    shape = (2, ATOM, VECS)
    first = vectors_ref[...].reshape(shape) * keep_of(widths, shape, 1)
    send_forms(first, plain_ref, flip_ref)


def applied(widths, own_ref, back_ref):
    shape = (2, ATOM, VECS)
    total = back_ref[...]
    for k in range(8):
        total = total + own_ref[k].astype(F32)
    return total.reshape(shape) * keep_of(widths, shape, 1)


def second_kernel(widths, own_ref, back_ref, vectors_ref, out_ref, plain_ref, flip_ref):
    shape = (2, ATOM, VECS)
    first = vectors_ref[...].reshape(shape) * keep_of(widths, shape, 1)
    second = applied(widths, own_ref, back_ref) - CENTER * first
    out_ref[...] = second.reshape(2 * ATOM, VECS)
    send_forms(second, plain_ref, flip_ref)


def last_kernel(widths, own_ref, back_ref, vectors_ref, second_ref, out_ref):
    shape = (2, ATOM, VECS)
    first = vectors_ref[...].reshape(shape) * keep_of(widths, shape, 1)
    third = applied(widths, own_ref, back_ref)
    out = 2.0 * (third - CENTER * second_ref[...].reshape(shape)) - first
    out_ref[...] = out.reshape(2 * ATOM, VECS)


def piece_at(place, i):
    y, xl = i // 2, i % 2
    return 2 * jnp.bitwise_and(y - place[1] + 4, 3) + xl


def device_of(place, k):
    return 2 * jnp.bitwise_and(k // 2 + place[1], 3) + k % 2


def stored(t_ref, e):
    block = t_ref[jnp.maximum(e, 0)]
    return jnp.where(e >= 0, block, jnp.zeros_like(block))


def direct_kernel(lists, slots, place, x_ref, t_ref, mine_ref, other_ref, held):
    co = place[0]
    for i in range(8):
        held[pl.ds(2 * piece_at(place, i), 2)] = x_ref[i].reshape(2, ATOM, VECS)

    def step(xz, carry):
        for t in range(2):
            length = 9 + t
            left = []
            for core in (co, 1 - co):
                at = (4 * xz + 2 * core + t) * D_LEN
                blocks = [stored(t_ref, slots[at + q]) for q in range(length)]
                left.append(jnp.concatenate(blocks, 1))
            right = [held[lists[(2 * xz + t) * D_LEN + q]] for q in range(length)]
            total = jnp.dot(
                jnp.concatenate(left, 0),
                jnp.concatenate(right, 0),
                preferred_element_type=F32,
            )
            rows = slice(t * ATOM, (t + 1) * ATOM)
            mine_ref[xz, rows, :] = total[:ATOM]
            other_ref[xz, rows, :] = total[ATOM:].astype(BF)
        return carry

    lax.fori_loop(0, 8, step, 0, unroll=True)


def mirror_kernel(lists, slots, place, x_ref, y_ref, t_ref, out_ref, held):
    co = place[0]
    for xz in range(8):
        held[pl.ds(4 * xz + 2 * co, 2)] = x_ref[xz]
        held[pl.ds(4 * xz + 2 - 2 * co, 2)] = y_ref[xz]

    def step(k, carry):
        for t in range(2):
            length = 18 - t
            left = [held[lists[(2 * k + t) * M_LEN + q]] for q in range(length)]
            right = []
            for b in (4 * k + t, 4 * k + 2 + t):
                blocks = [stored(t_ref, slots[b * M_LEN + q]) for q in range(length)]
                right.append(jnp.concatenate(blocks, 0))
            total = jnp.dot(
                jnp.concatenate(left, 1),
                jnp.concatenate(right, 1),
                preferred_element_type=F32,
            ).astype(BF)
            out_ref[device_of(place, 2 * k), t] = total[:, :ATOM]
            out_ref[device_of(place, 2 * k + 1), t] = total[:, ATOM:]
        return carry

    lax.fori_loop(0, 4, step, 0, unroll=True)


def gathered_kernel(got_ref, out_ref):
    total = got_ref[0].astype(F32)
    for i in range(1, 8):
        total = total + got_ref[i].astype(F32)
    out_ref[...] = total.astype(out_ref.dtype)


def turned_kernel(sum_ref, out_ref):
    out_ref[...] = jnp.swapaxes(sum_ref[...].astype(F32), 1, 2).reshape(2 * ATOM, VECS)


def both_kernel(mine_ref, theirs_ref, out_ref):
    out_ref[...] = (mine_ref[...] + theirs_ref[...].astype(F32)).astype(BF)


SMEM = pl.BlockSpec(memory_space=pltpu.SMEM)
VMEM = pl.BlockSpec(memory_space=pltpu.VMEM)
PARAMS = pltpu.CompilerParams(vmem_limit_bytes=24 * 1024 * 1024)
PIECE = (2 * ATOM, VECS)
BLOCKS = (2, ATOM, VECS)


def like(shape, dtype):
    return jax.ShapeDtypeStruct(shape, dtype)


def call(kernel, out_shape, scalars, arrays, scratch=(), flops=0, size=2**20, name=None):
    single = not isinstance(out_shape, tuple)
    return pl.pallas_call(
        kernel,
        out_shape=out_shape,
        in_specs=[SMEM] * len(scalars) + [VMEM] * len(arrays),
        out_specs=VMEM if single else (VMEM,) * len(out_shape),
        scratch_shapes=list(scratch),
        compiler_params=PARAMS,
        cost_estimate=pl.CostEstimate(flops=flops, bytes_accessed=size, transcendentals=0),
        name=name,
    )(*scalars, *arrays)


def shift_of(column):
    r = column // 2
    return (r // 2 - r % 4 + 2 * (column % 2)) % 4


def owners(r, c):
    column = 2 * r + c // 8
    y, xl = (c % 8 // 2 + shift_of(column)) % 4, c % 2
    return (2 * y + xl) * 16 + column


TO_COL = [(r * 16 + c, owners(r, c)) for r in range(8) for c in range(16)]
TO_ROW = [(d, s) for s, d in TO_COL]
SWAP = [(0, 1), (1, 0)]


def local(vectors, widths, tiles, block_rows, block_cols, block_count):
    row = lax.axis_index(ROWS)
    col = lax.axis_index(COLS)
    place = jnp.stack([lax.axis_index("co"), shift_of(col)]).astype(jnp.int32)
    tile_set = tiles[0, 0]
    direct_lists, direct_slots, mirror_lists, mirror_slots = tables(
        block_rows[0, 0], block_cols[0, 0], block_count[0, 0], row, col
    )
    work = dict(flops=2 * SLOTS * ATOM**3, size=2**23)

    def exchange(x, axes):
        return lax.all_to_all(x, axes, split_axis=0, concat_axis=0, tiled=True)

    def apply_matrix(plain, flipped, sent):
        piece = lax.ppermute(plain, ALL, TO_COL)
        near = exchange(flipped, ("xh", "z"))
        piece, near = lax.optimization_barrier((piece, near))
        far = lax.ppermute(near, "co", SWAP)
        col_block = exchange(jnp.broadcast_to(piece[None], (8, *PIECE)), ROWS)
        mirror = call(
            mirror_kernel,
            like((8, *BLOCKS), BF),
            (mirror_lists, mirror_slots, place),
            (near, far, tile_set),
            [pltpu.VMEM((AR, VECS, ATOM), BF)],
            name="mirror",
            **work,
        )
        col_block, mirror = lax.optimization_barrier((col_block, mirror))
        got = exchange(mirror, ROWS)
        mine, other = call(
            direct_kernel,
            (like((8, *PIECE), F32), like((8, *PIECE), BF)),
            (direct_lists, direct_slots, place),
            (col_block, tile_set),
            [pltpu.VMEM((AC, ATOM, VECS), BF)],
            name="direct",
            **work,
        )
        other, got = lax.optimization_barrier((other, got))
        theirs = lax.ppermute(other, "co", SWAP)
        both = call(both_kernel, like((8, *PIECE), BF), (), (mine, theirs), name="both")
        own = exchange(both, ("xh", "z"))
        gathered = call(gathered_kernel, like(BLOCKS, sent), (), (got,), name="gathered")
        back = lax.ppermute(gathered, ALL, TO_ROW)
        turned = call(turned_kernel, like(PIECE, F32), (), (back,), name="turned")
        return own, turned

    forms = (like(PIECE, BF), like((8, *BLOCKS), BF))
    plain, flipped = call(first_kernel, forms, (widths,), (vectors,), name="first")
    parts = apply_matrix(plain, flipped, F32)
    second, plain, flipped = call(
        second_kernel, (like(PIECE, F32), *forms), (widths,), (*parts, vectors), name="second"
    )
    parts = apply_matrix(plain, flipped, BF)
    return call(
        last_kernel, like(PIECE, F32), (widths,), (*parts, vectors, second), name="last"
    )

def solution(mesh):
    split = Mesh(mesh.devices.reshape(4, 2, 2, 4, 2), ALL)
    return jax.shard_map(
        local,
        mesh=split,
        in_specs=(
            P(ALL, None),
            P(ALL),
            P(ROWS, COLS, None, None, None),
            P(ROWS, COLS, None),
            P(ROWS, COLS, None),
            P(ROWS, COLS),
        ),
        out_specs=P(ALL, None),
        check_vma=False,
    )
```

```python
import functools

import jax
import jax.numpy as jnp
from jax import lax
from jax.experimental import pallas as pl
from jax.experimental.pallas import tpu as pltpu
from jax.sharding import Mesh
from jax.sharding import PartitionSpec as P

CENTER = 0.25
ATOM = 128
VECS = 128
AR = 32
AC = 16
SLOTS = 256
N_ROW = 8
N_COL = 16
BF = jnp.bfloat16
F32 = jnp.float32
ROWS = ("y", "xl")
COLS = ("xh", "z", "co")
ALL = ROWS + COLS
D_LEN = 9
M_LEN = 17


def tables(slot_rows, slot_cols, count, row, col):
    place = jnp.where(jnp.arange(SLOTS) < count, slot_rows * AC + slot_cols, -1)

    def pack(rows, cols, index, zero):
        want = (rows * AC + cols).reshape(-1, 1)
        entry = jnp.arange(SLOTS)[None, :] * 64 + index.reshape(-1, 1) - zero
        return zero + jnp.sum(jnp.where(place[None, :] == want, entry, 0), axis=1)

    a = jnp.arange(AR)[:, None]
    q = jnp.arange(D_LEN)[None, :]
    ga = row * AR + a
    gb = col * AC + 2 * q
    odd = ga % 2 == 1
    main = 2 * q + jnp.where(odd, ga <= gb + 1, ga > gb).astype(jnp.int32)
    extra = ga - 1 - col * AC
    extra = jnp.where(odd & (extra >= 0) & (extra < AC), extra, -AC * AR)
    b = jnp.where(q < 8, main, extra)
    direct = pack(a + 0 * b, b, b, AC)

    b = jnp.arange(AC)[:, None]
    q = jnp.arange(M_LEN)[None, :]
    gb = col * AC + b
    ga = row * AR + 2 * q
    odd = gb % 2 == 1
    main = 2 * q + jnp.where(odd, ga + 1 <= gb, ga > gb).astype(jnp.int32)
    extra = gb + 1 - row * AR
    extra = jnp.where((~odd) & (extra >= 0) & (extra < AR), extra, -AR)
    a = jnp.where(q < 16, main, extra)
    mirror = pack(a, b + 0 * a, a, AR)
    return direct, mirror


def keep_of(widths, shape, axis):
    place = lax.broadcasted_iota(jnp.int32, shape, axis)
    atom = lax.broadcasted_iota(jnp.int32, shape, 0)
    return (place < jnp.where(atom == 0, widths[0], widths[1])).astype(F32)


def send_forms(current, plain_ref, flip_ref):
    plain_ref[...] = current.reshape(2 * ATOM, VECS).astype(BF)
    flip_ref[...] = jnp.swapaxes(current, 1, 2).astype(BF)


def first_kernel(widths, vectors_ref, plain_ref, flip_ref):
    shape = (2, ATOM, VECS)
    first = vectors_ref[...].reshape(shape) * keep_of(widths, shape, 1)
    send_forms(first, plain_ref, flip_ref)


def applied(widths, own_ref, back_ref):
    shape = (2, ATOM, VECS)
    total = back_ref[...]
    for k in range(8):
        total = total + own_ref[k].astype(F32)
    return total.reshape(shape) * keep_of(widths, shape, 1)


def second_kernel(widths, own_ref, back_ref, vectors_ref, out_ref, plain_ref, flip_ref):
    shape = (2, ATOM, VECS)
    first = vectors_ref[...].reshape(shape) * keep_of(widths, shape, 1)
    second = applied(widths, own_ref, back_ref) - CENTER * first
    out_ref[...] = second.reshape(2 * ATOM, VECS)
    send_forms(second, plain_ref, flip_ref)


def last_kernel(widths, own_ref, back_ref, vectors_ref, second_ref, out_ref):
    shape = (2, ATOM, VECS)
    first = vectors_ref[...].reshape(shape) * keep_of(widths, shape, 1)
    third = applied(widths, own_ref, back_ref)
    out = 2.0 * (third - CENTER * second_ref[...].reshape(shape)) - first
    out_ref[...] = out.reshape(2 * ATOM, VECS)


def piece_at(place, i):
    y, xl = i // 2, i % 2
    return 2 * jnp.bitwise_and(y - place[1] + 4, 3) + xl


def direct_kernel(tab, place, x_ref, t_ref, mine_ref, other_ref, held):
    co = place[0]
    for i in range(8):
        held[pl.ds(2 * piece_at(place, i), 2)] = x_ref[i].reshape(2, ATOM, VECS)
    held[AC] = jnp.zeros((ATOM, VECS), BF)

    def product(a, q, n):
        blocks, xs = [], []
        for k in range(n):
            e = tab[a * D_LEN + q + k]
            blocks.append(t_ref[lax.shift_right_logical(e, 6)])
            xs.append(held[jnp.bitwise_and(e, 63)])
        if n == 1:
            left, right = blocks[0], xs[0]
        else:
            left, right = jnp.concatenate(blocks, 1), jnp.concatenate(xs, 0)
        return jnp.dot(left, right, preferred_element_type=F32)

    def step(xz, carry):
        for which, out in ((0, mine_ref), (1, other_ref)):
            for t in range(2):
                a = 4 * xz + 2 * (co if which == 0 else 1 - co) + t
                total = product(a, 0, 8)
                if t:
                    total = total + product(a, 8, 1)
                out[xz, t * ATOM:(t + 1) * ATOM, :] = total.astype(out.dtype)
        return carry

    lax.fori_loop(0, 8, step, 0, unroll=True)


def mirror_kernel(tab, place, z0_ref, z1_ref, z2_ref, z3_ref, c0_ref, c1_ref, c2_ref, c3_ref,
                  t_ref, out_ref, held):
    co, z, xh = place[0], place[2], place[3]
    for core, refs in (
        (co, (z0_ref, z1_ref, z2_ref, z3_ref)),
        (1 - co, (c0_ref, c1_ref, c2_ref, c3_ref)),
    ):
        for s, ref in enumerate(refs):
            for rel in range(2):
                c = 8 * jnp.bitwise_xor(xh, rel) + 2 * jnp.bitwise_and(z - s + 4, 3) + core
                held[pl.ds(2 * c, 2)] = ref[rel]
    held[AR] = jnp.zeros((VECS, ATOM), BF)

    def product(b, q, n):
        blocks, xs = [], []
        for k in range(n):
            e = tab[b * M_LEN + q + k]
            blocks.append(t_ref[lax.shift_right_logical(e, 6)])
            xs.append(held[jnp.bitwise_and(e, 63)])
        if n == 1:
            left, right = xs[0], blocks[0]
        else:
            left, right = jnp.concatenate(xs, 1), jnp.concatenate(blocks, 0)
        return jnp.dot(left, right, preferred_element_type=F32)

    def step(i, carry):
        k = piece_at(place, i)
        for t in range(2):
            b = 2 * k + t
            total = product(b, 0, 8) + product(b, 8, 8)
            if not t:
                total = total + product(b, 16, 1)
            out_ref[i, t] = total.astype(out_ref.dtype)
        return carry

    lax.fori_loop(0, 8, step, 0, unroll=True)


def gathered_kernel(got_ref, out_ref):
    total = got_ref[0].astype(F32)
    for i in range(1, 8):
        total = total + got_ref[i].astype(F32)
    out_ref[...] = total.astype(out_ref.dtype)


def turned_kernel(sum_ref, out_ref):
    out_ref[...] = jnp.swapaxes(sum_ref[...].astype(F32), 1, 2).reshape(2 * ATOM, VECS)


def both_kernel(mine_ref, theirs_ref, out_ref):
    out_ref[...] = (mine_ref[...] + theirs_ref[...].astype(F32)).astype(BF)


SMEM = pl.BlockSpec(memory_space=pltpu.SMEM)
VMEM = pl.BlockSpec(memory_space=pltpu.VMEM)
PARAMS = pltpu.CompilerParams(vmem_limit_bytes=24 * 1024 * 1024)
PIECE = (2 * ATOM, VECS)
BLOCKS = (2, ATOM, VECS)


def like(shape, dtype):
    return jax.ShapeDtypeStruct(shape, dtype)


def call(kernel, out_shape, scalars, arrays, scratch=(), flops=0, size=2**20, name=None):
    single = not isinstance(out_shape, tuple)
    return pl.pallas_call(
        kernel,
        out_shape=out_shape,
        in_specs=[SMEM] * len(scalars) + [VMEM] * len(arrays),
        out_specs=VMEM if single else (VMEM,) * len(out_shape),
        scratch_shapes=list(scratch),
        compiler_params=PARAMS,
        cost_estimate=pl.CostEstimate(flops=flops, bytes_accessed=size, transcendentals=0),
        name=name,
    )(*scalars, *arrays)


def shift_of(column):
    r = column // 2
    return (r // 2 - r % 4 + 2 * (column % 2)) % 4


def owners(r, c):
    column = 2 * r + c // 8
    y, xl = (c % 8 // 2 + shift_of(column)) % 4, c % 2
    return (2 * y + xl) * 16 + column


TO_COL = [(r * 16 + c, owners(r, c)) for r in range(8) for c in range(16)]
TO_ROW = [(d, s) for s, d in TO_COL]
SWAP = [(0, 1), (1, 0)]


def turn(s):
    return [(k, (k + s) % 4) for k in range(4)]


def local(vectors, widths, tiles, block_rows, block_cols, block_count):
    row = lax.axis_index(ROWS)
    col = lax.axis_index(COLS)
    place = jnp.stack(
        [lax.axis_index("co"), shift_of(col), lax.axis_index("z"), lax.axis_index("xh")]
    ).astype(jnp.int32)
    tile_set = tiles[0, 0]
    direct_tab, mirror_tab = tables(
        block_rows[0, 0], block_cols[0, 0], block_count[0, 0], row, col
    )
    work = dict(flops=2 * SLOTS * ATOM**3, size=2**23)

    def exchange(x, axes):
        return lax.all_to_all(x, axes, split_axis=0, concat_axis=0, tiled=True)

    def apply_matrix(plain, flipped, sent):
        piece = lax.ppermute(plain, ALL, TO_COL)
        pair = jnp.stack([flipped, lax.ppermute(flipped, "xh", SWAP)])
        turns = [lax.ppermute(pair, "z", turn(s)) for s in (1, 2, 3)]
        piece, *turns = lax.optimization_barrier((piece, *turns))
        turns = [pair, *turns]
        crossed = [lax.ppermute(t, "co", SWAP) for t in turns]
        col_block = exchange(jnp.broadcast_to(piece[None], (8, *PIECE)), ROWS)
        mirror = call(
            mirror_kernel,
            like((8, *BLOCKS), BF),
            (mirror_tab, place),
            (*turns, *crossed, tile_set),
            [pltpu.VMEM((AR + 1, VECS, ATOM), BF)],
            name="mirror",
            **work,
        )
        col_block, mirror = lax.optimization_barrier((col_block, mirror))
        got = exchange(mirror, ROWS)
        mine, other = call(
            direct_kernel,
            (like((8, *PIECE), F32), like((8, *PIECE), BF)),
            (direct_tab, place),
            (col_block, tile_set),
            [pltpu.VMEM((AC + 1, ATOM, VECS), BF)],
            name="direct",
            **work,
        )
        other, got = lax.optimization_barrier((other, got))
        theirs = lax.ppermute(other, "co", SWAP)
        both = call(both_kernel, like((8, *PIECE), BF), (), (mine, theirs), name="both")
        own = exchange(both, ("xh", "z"))
        gathered = call(gathered_kernel, like(BLOCKS, sent), (), (got,), name="gathered")
        back = lax.ppermute(gathered, ALL, TO_ROW)
        turned = call(turned_kernel, like(PIECE, F32), (), (back,), name="turned")
        return own, turned

    forms = (like(PIECE, BF), like(BLOCKS, BF))
    plain, flipped = call(first_kernel, forms, (widths,), (vectors,), name="first")
    parts = apply_matrix(plain, flipped, F32)
    second, plain, flipped = call(
        second_kernel, (like(PIECE, F32), *forms), (widths,), (*parts, vectors), name="second"
    )
    parts = apply_matrix(plain, flipped, BF)
    return call(
        last_kernel, like(PIECE, F32), (widths,), (*parts, vectors, second), name="last"
    )

def solution(mesh):
    split = Mesh(mesh.devices.reshape(4, 2, 2, 4, 2), ALL)
    return jax.shard_map(
        local,
        mesh=split,
        in_specs=(
            P(ALL, None),
            P(ALL),
            P(ROWS, COLS, None, None, None),
            P(ROWS, COLS, None),
            P(ROWS, COLS, None),
            P(ROWS, COLS),
        ),
        out_specs=P(ALL, None),
        check_vma=False,
    )
```

```python
import functools

import jax
import jax.numpy as jnp
from jax import lax
from jax.experimental import pallas as pl
from jax.experimental.pallas import tpu as pltpu
from jax.sharding import Mesh
from jax.sharding import PartitionSpec as P

CENTER = 0.25
ATOM = 128
VECS = 128
AR = 32
AC = 16
SLOTS = 256
N_ROW = 8
N_COL = 16
BF = jnp.bfloat16
F32 = jnp.float32
ROWS = ("y", "xl")
COLS = ("xh", "z", "co")
ALL = ROWS + COLS
D_LEN = 9
M_LEN = 17
PIECE = (2 * ATOM, VECS)
BLOCKS = (2, ATOM, VECS)


def tables(slot_rows, slot_cols, count, row, col):
    place = jnp.where(jnp.arange(SLOTS) < count, slot_rows * AC + slot_cols, -1)

    def pack(rows, cols, index, zero):
        want = (rows * AC + cols).reshape(-1, 1)
        entry = jnp.arange(SLOTS)[None, :] * 64 + index.reshape(-1, 1) - zero
        return zero + jnp.sum(jnp.where(place[None, :] == want, entry, 0), axis=1)

    a = jnp.arange(AR)[:, None]
    q = jnp.arange(D_LEN)[None, :]
    ga = row * AR + a
    gb = col * AC + 2 * q
    odd = ga % 2 == 1
    main = 2 * q + jnp.where(odd, ga <= gb + 1, ga > gb).astype(jnp.int32)
    extra = ga - 1 - col * AC
    extra = jnp.where(odd & (extra >= 0) & (extra < AC), extra, -AC * AR)
    b = jnp.where(q < 8, main, extra)
    direct = pack(a + 0 * b, b, b, AC)

    b = jnp.arange(AC)[:, None]
    q = jnp.arange(M_LEN)[None, :]
    gb = col * AC + b
    ga = row * AR + 2 * q
    odd = gb % 2 == 1
    main = 2 * q + jnp.where(odd, ga + 1 <= gb, ga > gb).astype(jnp.int32)
    extra = gb + 1 - row * AR
    extra = jnp.where((~odd) & (extra >= 0) & (extra < AR), extra, -AR)
    a = jnp.where(q < 16, main, extra)
    mirror = pack(a, b + 0 * a, a, AR)
    return direct, mirror


def keep_of(widths, shape, axis):
    place = lax.broadcasted_iota(jnp.int32, shape, axis)
    atom = lax.broadcasted_iota(jnp.int32, shape, 0)
    return (place < jnp.where(atom == 0, widths[0], widths[1])).astype(F32)


def spread(block_ref, copies_ref, sem):
    copies = [
        pltpu.make_async_copy(block_ref, copies_ref.at[k], sem.at[k]) for k in range(8)
    ]
    for copy in copies:
        copy.start()
    return copies


def send_forms(current, plain_ref, flip_ref, block, sem):
    block[...] = jnp.swapaxes(current, 1, 2).astype(BF)
    copies = spread(block, flip_ref, sem)
    plain_ref[...] = current.reshape(2 * ATOM, VECS).astype(BF)
    return copies


def first_kernel(widths, vectors_ref, plain_ref, flip_ref, block, sem):
    first = vectors_ref[...].reshape(BLOCKS) * keep_of(widths, BLOCKS, 1)
    for copy in send_forms(first, plain_ref, flip_ref, block, sem):
        copy.wait()


def applied(widths, own_ref, back_ref):
    total = jnp.swapaxes(back_ref[...], 1, 2).reshape(2 * ATOM, VECS)
    for k in range(8):
        total = total + own_ref[k].astype(F32)
    return total.reshape(BLOCKS) * keep_of(widths, BLOCKS, 1)


def second_kernel(
    widths, own_ref, back_ref, vectors_ref, out_ref, plain_ref, flip_ref, block, sem
):
    first = vectors_ref[...].reshape(BLOCKS) * keep_of(widths, BLOCKS, 1)
    second = applied(widths, own_ref, back_ref) - CENTER * first
    copies = send_forms(second, plain_ref, flip_ref, block, sem)
    out_ref[...] = second.reshape(2 * ATOM, VECS)
    for copy in copies:
        copy.wait()


def last_kernel(widths, own_ref, back_ref, vectors_ref, second_ref, out_ref):
    first = vectors_ref[...].reshape(BLOCKS) * keep_of(widths, BLOCKS, 1)
    third = applied(widths, own_ref, back_ref)
    out = 2.0 * (third - CENTER * second_ref[...].reshape(BLOCKS)) - first
    out_ref[...] = out.reshape(2 * ATOM, VECS)


def copies_kernel(piece_ref, out_ref, sem):
    for copy in spread(piece_ref, out_ref, sem):
        copy.wait()


def piece_at(place, i):
    y, xl = i // 2, i % 2
    return 2 * jnp.bitwise_and(y - place[1] + 4, 3) + xl


def direct_kernel(tab, place, x_ref, t_ref, mine_ref, other_ref, held):
    co = place[0]
    for i in range(8):
        held[pl.ds(2 * piece_at(place, i), 2)] = x_ref[i].reshape(2, ATOM, VECS)
    held[AC] = jnp.zeros((ATOM, VECS), BF)

    def product(a, q, n):
        blocks, xs = [], []
        for k in range(n):
            e = tab[a * D_LEN + q + k]
            blocks.append(t_ref[lax.shift_right_logical(e, 6)])
            xs.append(held[jnp.bitwise_and(e, 63)])
        if n == 1:
            left, right = blocks[0], xs[0]
        else:
            left, right = jnp.concatenate(blocks, 1), jnp.concatenate(xs, 0)
        return jnp.dot(left, right, preferred_element_type=F32)

    def step(xz, carry):
        for which, out in ((0, mine_ref), (1, other_ref)):
            for t in range(2):
                a = 4 * xz + 2 * (co if which == 0 else 1 - co) + t
                total = product(a, 0, 8)
                if t:
                    total = total + product(a, 8, 1)
                out[xz, t * ATOM:(t + 1) * ATOM, :] = total.astype(out.dtype)
        return carry

    lax.fori_loop(0, 8, step, 0, unroll=True)


def mirror_kernel(tab, place, x_ref, y_ref, t_ref, out_ref, held):
    co = place[0]
    for xz in range(8):
        held[pl.ds(4 * xz + 2 * co, 2)] = x_ref[xz]
        held[pl.ds(4 * xz + 2 - 2 * co, 2)] = y_ref[xz]
    held[AR] = jnp.zeros((VECS, ATOM), BF)

    def product(b, q, n):
        blocks, xs = [], []
        for k in range(n):
            e = tab[b * M_LEN + q + k]
            blocks.append(t_ref[lax.shift_right_logical(e, 6)])
            xs.append(held[jnp.bitwise_and(e, 63)])
        if n == 1:
            left, right = xs[0], blocks[0]
        else:
            left, right = jnp.concatenate(xs, 1), jnp.concatenate(blocks, 0)
        return jnp.dot(left, right, preferred_element_type=F32)

    def step(i, carry):
        k = piece_at(place, i)
        for t in range(2):
            b = 2 * k + t
            total = product(b, 0, 8) + product(b, 8, 8)
            if not t:
                total = total + product(b, 16, 1)
            out_ref[i, t] = total.astype(out_ref.dtype)
        return carry

    lax.fori_loop(0, 8, step, 0, unroll=True)


def gathered_kernel(got_ref, out_ref):
    total = got_ref[0].astype(F32)
    for i in range(1, 8):
        total = total + got_ref[i].astype(F32)
    out_ref[...] = total.astype(out_ref.dtype)


def both_kernel(mine_ref, theirs_ref, out_ref):
    out_ref[...] = (mine_ref[...] + theirs_ref[...].astype(F32)).astype(BF)


SMEM = pl.BlockSpec(memory_space=pltpu.SMEM)
VMEM = pl.BlockSpec(memory_space=pltpu.VMEM)
PARAMS = pltpu.CompilerParams(vmem_limit_bytes=24 * 1024 * 1024)
ANY = pl.BlockSpec(memory_space=pl.ANY)


def like(shape, dtype):
    return jax.ShapeDtypeStruct(shape, dtype)


def call(
    kernel, out_shape, scalars, arrays, scratch=(), flops=0, size=2**20, name=None, outs=None
):
    single = not isinstance(out_shape, tuple)
    return pl.pallas_call(
        kernel,
        out_shape=out_shape,
        in_specs=[SMEM] * len(scalars) + [VMEM] * len(arrays),
        out_specs=outs or (VMEM if single else (VMEM,) * len(out_shape)),
        scratch_shapes=list(scratch),
        compiler_params=PARAMS,
        cost_estimate=pl.CostEstimate(flops=flops, bytes_accessed=size, transcendentals=0),
        name=name,
    )(*scalars, *arrays)


def shift_of(column):
    r = column // 2
    return (r // 2 - r % 4 + 2 * (column % 2)) % 4


def owners(r, c):
    column = 2 * r + c // 8
    y, xl = (c % 8 // 2 + shift_of(column)) % 4, c % 2
    return (2 * y + xl) * 16 + column


TO_COL = [(r * 16 + c, owners(r, c)) for r in range(8) for c in range(16)]
TO_ROW = [(d, s) for s, d in TO_COL]
SWAP = [(0, 1), (1, 0)]


def local(vectors, widths, tiles, block_rows, block_cols, block_count):
    row = lax.axis_index(ROWS)
    col = lax.axis_index(COLS)
    place = jnp.stack([lax.axis_index("co"), shift_of(col)]).astype(jnp.int32)
    tile_set = tiles[0, 0]
    direct_tab, mirror_tab = tables(
        block_rows[0, 0], block_cols[0, 0], block_count[0, 0], row, col
    )
    work = dict(flops=2 * SLOTS * ATOM**3, size=2**23)

    def exchange(x, axes):
        return lax.all_to_all(x, axes, split_axis=0, concat_axis=0, tiled=True)

    def copies(piece):
        return call(
            copies_kernel,
            like((8, *PIECE), BF),
            (),
            (piece,),
            [pltpu.SemaphoreType.DMA((8,))],
            name="copies",
            outs=ANY,
        )

    def apply_matrix(plain, flipped):
        piece = lax.ppermute(plain, ALL, TO_COL)
        near = exchange(flipped, ("xh", "z"))
        piece, near = lax.optimization_barrier((piece, near))
        far = lax.ppermute(near, "co", SWAP)
        col_block = exchange(copies(piece), ROWS)
        mirror = call(
            mirror_kernel,
            like((8, *BLOCKS), BF),
            (mirror_tab, place),
            (near, far, tile_set),
            [pltpu.VMEM((AR + 1, VECS, ATOM), BF)],
            name="mirror",
            **work,
        )
        col_block, mirror = lax.optimization_barrier((col_block, mirror))
        got = exchange(mirror, ROWS)
        mine, other = call(
            direct_kernel,
            (like((8, *PIECE), F32), like((8, *PIECE), BF)),
            (direct_tab, place),
            (col_block, tile_set),
            [pltpu.VMEM((AC + 1, ATOM, VECS), BF)],
            name="direct",
            **work,
        )
        other, got = lax.optimization_barrier((other, got))
        theirs = lax.ppermute(other, "co", SWAP)
        both = call(both_kernel, like((8, *PIECE), BF), (), (mine, theirs), name="both")
        own = exchange(both, ("xh", "z"))
        gathered = call(gathered_kernel, like(BLOCKS, F32), (), (got,), name="gathered")
        back = lax.ppermute(gathered, ALL, TO_ROW)
        return own, back

    forms = (like(PIECE, BF), like((8, *BLOCKS), BF))
    sent = [pltpu.VMEM(BLOCKS, BF), pltpu.SemaphoreType.DMA((8,))]
    plain, flipped = call(
        first_kernel, forms, (widths,), (vectors,), sent, name="first", outs=(VMEM, ANY)
    )
    parts = apply_matrix(plain, flipped)
    second, plain, flipped = call(
        second_kernel,
        (like(PIECE, F32), *forms),
        (widths,),
        (*parts, vectors),
        sent,
        name="second",
        outs=(VMEM, VMEM, ANY),
    )
    parts = apply_matrix(plain, flipped)
    return call(
        last_kernel, like(PIECE, F32), (widths,), (*parts, vectors, second), name="last"
    )

def solution(mesh):
    split = Mesh(mesh.devices.reshape(4, 2, 2, 4, 2), ALL)
    return jax.shard_map(
        local,
        mesh=split,
        in_specs=(
            P(ALL, None),
            P(ALL),
            P(ROWS, COLS, None, None, None),
            P(ROWS, COLS, None),
            P(ROWS, COLS, None),
            P(ROWS, COLS),
        ),
        out_specs=P(ALL, None),
        check_vma=False,
    )
```

```python
import functools

import jax
import jax.numpy as jnp
from jax import lax
from jax.experimental import pallas as pl
from jax.experimental.pallas import tpu as pltpu
from jax.sharding import Mesh
from jax.sharding import PartitionSpec as P

CENTER = 0.25
ATOM = 128
VECS = 128
AR = 32
AC = 16
SLOTS = 256
N_ROW = 8
N_COL = 16
BF = jnp.bfloat16
F32 = jnp.float32
ROWS = ("y", "xl")
COLS = ("xh", "z", "co")
ALL = ROWS + COLS
D_LEN = 9
M_LEN = 17


def tables(slot_rows, slot_cols, count, row, col):
    place = jnp.where(jnp.arange(SLOTS) < count, slot_rows * AC + slot_cols, -1)

    def pack(rows, cols, index, zero):
        want = (rows * AC + cols).reshape(-1, 1)
        entry = jnp.arange(SLOTS)[None, :] * 64 + index.reshape(-1, 1) - zero
        return zero + jnp.sum(jnp.where(place[None, :] == want, entry, 0), axis=1)

    a = jnp.arange(AR)[:, None]
    q = jnp.arange(D_LEN)[None, :]
    ga = row * AR + a
    gb = col * AC + 2 * q
    odd = ga % 2 == 1
    main = 2 * q + jnp.where(odd, ga <= gb + 1, ga > gb).astype(jnp.int32)
    extra = ga - 1 - col * AC
    extra = jnp.where(odd & (extra >= 0) & (extra < AC), extra, -AC * AR)
    b = jnp.where(q < 8, main, extra)
    direct = pack(a + 0 * b, b, b, AC)

    b = jnp.arange(AC)[:, None]
    q = jnp.arange(M_LEN)[None, :]
    gb = col * AC + b
    ga = row * AR + 2 * q
    odd = gb % 2 == 1
    main = 2 * q + jnp.where(odd, ga + 1 <= gb, ga > gb).astype(jnp.int32)
    extra = gb + 1 - row * AR
    extra = jnp.where((~odd) & (extra >= 0) & (extra < AR), extra, -AR)
    a = jnp.where(q < 16, main, extra)
    mirror = pack(a, b + 0 * a, a, AR)
    return direct, mirror


def keep_of(widths, shape, axis):
    place = lax.broadcasted_iota(jnp.int32, shape, axis)
    atom = lax.broadcasted_iota(jnp.int32, shape, 0)
    return (place < jnp.where(atom == 0, widths[0], widths[1])).astype(F32)


def send_forms(current, plain_ref, flip_ref):
    plain_ref[...] = current.reshape(2 * ATOM, VECS).astype(BF)
    flipped = jnp.swapaxes(current, 1, 2).astype(BF)
    for k in range(8):
        flip_ref[k] = flipped


def first_kernel(widths, vectors_ref, plain_ref, flip_ref):
    shape = (2, ATOM, VECS)
    first = vectors_ref[...].reshape(shape) * keep_of(widths, shape, 1)
    send_forms(first, plain_ref, flip_ref)


def applied(widths, own_ref, back_ref):
    shape = (2, ATOM, VECS)
    total = back_ref[...]
    for k in range(8):
        total = total + own_ref[k].astype(F32)
    return total.reshape(shape) * keep_of(widths, shape, 1)


def second_kernel(widths, own_ref, back_ref, vectors_ref, out_ref, plain_ref, flip_ref):
    shape = (2, ATOM, VECS)
    first = vectors_ref[...].reshape(shape) * keep_of(widths, shape, 1)
    second = applied(widths, own_ref, back_ref) - CENTER * first
    out_ref[...] = second.reshape(2 * ATOM, VECS)
    send_forms(second, plain_ref, flip_ref)


def last_kernel(widths, own_ref, back_ref, vectors_ref, second_ref, out_ref):
    shape = (2, ATOM, VECS)
    first = vectors_ref[...].reshape(shape) * keep_of(widths, shape, 1)
    third = applied(widths, own_ref, back_ref)
    out = 2.0 * (third - CENTER * second_ref[...].reshape(shape)) - first
    out_ref[...] = out.reshape(2 * ATOM, VECS)


def piece_at(place, i):
    y, xl = i // 2, i % 2
    return 2 * jnp.bitwise_and(y - place[1] + 4, 3) + xl


def direct_kernel(tab, place, x_ref, t_ref, mine_ref, other_ref, held):
    co = place[0]
    for i in range(8):
        held[pl.ds(2 * piece_at(place, i), 2)] = x_ref[i].reshape(2, ATOM, VECS)
    held[AC] = jnp.zeros((ATOM, VECS), BF)

    def product(a, q, n):
        blocks, xs = [], []
        for k in range(n):
            e = tab[a * D_LEN + q + k]
            blocks.append(t_ref[lax.shift_right_logical(e, 6)])
            xs.append(held[jnp.bitwise_and(e, 63)])
        if n == 1:
            left, right = blocks[0], xs[0]
        else:
            left, right = jnp.concatenate(blocks, 1), jnp.concatenate(xs, 0)
        return jnp.dot(left, right, preferred_element_type=F32)

    def step(xz, carry):
        for which, out in ((0, mine_ref), (1, other_ref)):
            for t in range(2):
                a = 4 * xz + 2 * (co if which == 0 else 1 - co) + t
                total = product(a, 0, 8)
                if t:
                    total = total + product(a, 8, 1)
                out[xz, t * ATOM:(t + 1) * ATOM, :] = total.astype(out.dtype)
        return carry

    lax.fori_loop(0, 8, step, 0, unroll=True)


def mirror_kernel(tab, place, x_ref, y_ref, t_ref, out_ref, held):
    co = place[0]
    for xz in range(8):
        held[pl.ds(4 * xz + 2 * co, 2)] = x_ref[xz]
        held[pl.ds(4 * xz + 2 - 2 * co, 2)] = y_ref[xz]
    held[AR] = jnp.zeros((VECS, ATOM), BF)

    def product(b, q, n):
        blocks, xs = [], []
        for k in range(n):
            e = tab[b * M_LEN + q + k]
            blocks.append(t_ref[lax.shift_right_logical(e, 6)])
            xs.append(held[jnp.bitwise_and(e, 63)])
        if n == 1:
            left, right = xs[0], blocks[0]
        else:
            left, right = jnp.concatenate(xs, 1), jnp.concatenate(blocks, 0)
        return jnp.dot(left, right, preferred_element_type=F32)

    def step(i, carry):
        k = piece_at(place, i)
        for t in range(2):
            b = 2 * k + t
            total = product(b, 0, 8) + product(b, 8, 8)
            if not t:
                total = total + product(b, 16, 1)
            out_ref[i, t] = total.astype(out_ref.dtype)
        return carry

    lax.fori_loop(0, 8, step, 0, unroll=True)


def gathered_kernel(got_ref, out_ref):
    total = got_ref[0].astype(F32)
    for i in range(1, 8):
        total = total + got_ref[i].astype(F32)
    out_ref[...] = total.astype(out_ref.dtype)


def turned_kernel(sum_ref, out_ref):
    out_ref[...] = jnp.swapaxes(sum_ref[...].astype(F32), 1, 2).reshape(2 * ATOM, VECS)


def both_kernel(mine_ref, theirs_ref, out_ref):
    out_ref[...] = (mine_ref[...] + theirs_ref[...].astype(F32)).astype(BF)


SMEM = pl.BlockSpec(memory_space=pltpu.SMEM)
VMEM = pl.BlockSpec(memory_space=pltpu.VMEM)
PARAMS = pltpu.CompilerParams(vmem_limit_bytes=24 * 1024 * 1024)
PIECE = (2 * ATOM, VECS)
BLOCKS = (2, ATOM, VECS)


def like(shape, dtype):
    return jax.ShapeDtypeStruct(shape, dtype)


def call(kernel, out_shape, scalars, arrays, scratch=(), flops=0, size=2**20, name=None):
    single = not isinstance(out_shape, tuple)
    return pl.pallas_call(
        kernel,
        out_shape=out_shape,
        in_specs=[SMEM] * len(scalars) + [VMEM] * len(arrays),
        out_specs=VMEM if single else (VMEM,) * len(out_shape),
        scratch_shapes=list(scratch),
        compiler_params=PARAMS,
        cost_estimate=pl.CostEstimate(flops=flops, bytes_accessed=size, transcendentals=0),
        name=name,
    )(*scalars, *arrays)


def shift_of(column):
    r = column // 2
    return (r // 2 - r % 4 + 2 * (column % 2)) % 4


def owners(r, c):
    column = 2 * r + c // 8
    y, xl = (c % 8 // 2 + shift_of(column)) % 4, c % 2
    return (2 * y + xl) * 16 + column


TO_COL = [(r * 16 + c, owners(r, c)) for r in range(8) for c in range(16)]
TO_ROW = [(d, s) for s, d in TO_COL]
SWAP = [(0, 1), (1, 0)]


def local(vectors, widths, tiles, block_rows, block_cols, block_count):
    row = lax.axis_index(ROWS)
    col = lax.axis_index(COLS)
    place = jnp.stack([lax.axis_index("co"), shift_of(col)]).astype(jnp.int32)
    tile_set = tiles[0, 0]
    direct_tab, mirror_tab = tables(
        block_rows[0, 0], block_cols[0, 0], block_count[0, 0], row, col
    )
    work = dict(flops=2 * SLOTS * ATOM**3, size=2**23)

    def exchange(x, axes):
        return lax.all_to_all(x, axes, split_axis=0, concat_axis=0, tiled=True)

    def apply_matrix(plain, flipped):
        piece = lax.ppermute(plain, ALL, TO_COL)
        near = exchange(flipped, ("xh", "z"))
        piece, near = lax.optimization_barrier((piece, near))
        far = lax.ppermute(near, "co", SWAP)
        col_block = exchange(jnp.broadcast_to(piece[None], (8, *PIECE)), ROWS)
        mirror = call(
            mirror_kernel,
            like((8, *BLOCKS), BF),
            (mirror_tab, place),
            (near, far, tile_set),
            [pltpu.VMEM((AR + 1, VECS, ATOM), BF)],
            name="mirror",
            **work,
        )
        col_block, mirror = lax.optimization_barrier((col_block, mirror))
        got = exchange(mirror, ROWS)
        mine, other = call(
            direct_kernel,
            (like((8, *PIECE), F32), like((8, *PIECE), BF)),
            (direct_tab, place),
            (col_block, tile_set),
            [pltpu.VMEM((AC + 1, ATOM, VECS), BF)],
            name="direct",
            **work,
        )
        other, got = lax.optimization_barrier((other, got))
        theirs = lax.ppermute(other, "co", SWAP)
        both = call(both_kernel, like((8, *PIECE), BF), (), (mine, theirs), name="both")
        own = exchange(both, ("xh", "z"))
        gathered = call(gathered_kernel, like(BLOCKS, BF), (), (got,), name="gathered")
        back = lax.ppermute(gathered, ALL, TO_ROW)
        turned = call(turned_kernel, like(PIECE, F32), (), (back,), name="turned")
        return own, turned

    forms = (like(PIECE, BF), like((8, *BLOCKS), BF))
    plain, flipped = call(first_kernel, forms, (widths,), (vectors,), name="first")
    parts = apply_matrix(plain, flipped)
    second, plain, flipped = call(
        second_kernel, (like(PIECE, F32), *forms), (widths,), (*parts, vectors), name="second"
    )
    parts = apply_matrix(plain, flipped)
    return call(
        last_kernel, like(PIECE, F32), (widths,), (*parts, vectors, second), name="last"
    )

def solution(mesh):
    split = Mesh(mesh.devices.reshape(4, 2, 2, 4, 2), ALL)
    return jax.shard_map(
        local,
        mesh=split,
        in_specs=(
            P(ALL, None),
            P(ALL),
            P(ROWS, COLS, None, None, None),
            P(ROWS, COLS, None),
            P(ROWS, COLS, None),
            P(ROWS, COLS),
        ),
        out_specs=P(ALL, None),
        check_vma=False,
    )
```

```python
import functools

import jax
import jax.numpy as jnp
from jax import lax
from jax.experimental import pallas as pl
from jax.experimental.pallas import tpu as pltpu
from jax.sharding import Mesh
from jax.sharding import PartitionSpec as P

CENTER = 0.25
ATOM = 128
VECS = 128
AR = 32
AC = 16
SLOTS = 256
N_ROW = 8
N_COL = 16
BF = jnp.bfloat16
F32 = jnp.float32
ROWS = ("y", "xl")
COLS = ("xh", "z", "co")
ALL = ROWS + COLS
D_LEN = 9
M_LEN = 17


def tables(slot_rows, slot_cols, count, row, col):
    place = jnp.where(jnp.arange(SLOTS) < count, slot_rows * AC + slot_cols, -1)

    def pack(rows, cols, index, zero):
        want = (rows * AC + cols).reshape(-1, 1)
        entry = jnp.arange(SLOTS)[None, :] * 64 + index.reshape(-1, 1) - zero
        return zero + jnp.sum(jnp.where(place[None, :] == want, entry, 0), axis=1)

    a = jnp.arange(AR)[:, None]
    q = jnp.arange(D_LEN)[None, :]
    ga = row * AR + a
    gb = col * AC + 2 * q
    odd = ga % 2 == 1
    main = 2 * q + jnp.where(odd, ga <= gb + 1, ga > gb).astype(jnp.int32)
    extra = ga - 1 - col * AC
    extra = jnp.where(odd & (extra >= 0) & (extra < AC), extra, -AC * AR)
    b = jnp.where(q < 8, main, extra)
    direct = pack(a + 0 * b, b, b, AC)

    b = jnp.arange(AC)[:, None]
    q = jnp.arange(M_LEN)[None, :]
    gb = col * AC + b
    ga = row * AR + 2 * q
    odd = gb % 2 == 1
    main = 2 * q + jnp.where(odd, ga + 1 <= gb, ga > gb).astype(jnp.int32)
    extra = gb + 1 - row * AR
    extra = jnp.where((~odd) & (extra >= 0) & (extra < AR), extra, -AR)
    a = jnp.where(q < 16, main, extra)
    mirror = pack(a, b + 0 * a, a, AR)
    return direct, mirror


def keep_of(widths, shape, axis):
    place = lax.broadcasted_iota(jnp.int32, shape, axis)
    atom = lax.broadcasted_iota(jnp.int32, shape, 0)
    return (place < jnp.where(atom == 0, widths[0], widths[1])).astype(F32)


def send_forms(current, plain_ref, flip_ref):
    plain_ref[...] = current.reshape(2 * ATOM, VECS).astype(BF)
    flipped = jnp.swapaxes(current, 1, 2).astype(BF)
    for k in range(8):
        flip_ref[k] = flipped


def first_kernel(widths_ref, vectors_ref, plain_ref, flip_ref, widths, vectors, sem):
    copies = [
        pltpu.make_async_copy(vectors_ref, vectors, sem.at[0]),
        pltpu.make_async_copy(widths_ref, widths, sem.at[1]),
    ]
    for copy in copies:
        copy.start()
    for copy in copies:
        copy.wait()
    shape = (2, ATOM, VECS)
    first = vectors[...].reshape(shape) * keep_of(widths, shape, 1)
    send_forms(first, plain_ref, flip_ref)


def applied(widths, own_ref, back_ref):
    shape = (2, ATOM, VECS)
    total = back_ref[...]
    for k in range(8):
        total = total + own_ref[k].astype(F32)
    return total.reshape(shape) * keep_of(widths, shape, 1)


def second_kernel(widths, own_ref, back_ref, vectors_ref, out_ref, plain_ref, flip_ref):
    shape = (2, ATOM, VECS)
    first = vectors_ref[...].reshape(shape) * keep_of(widths, shape, 1)
    second = applied(widths, own_ref, back_ref) - CENTER * first
    out_ref[...] = second.reshape(2 * ATOM, VECS)
    send_forms(second, plain_ref, flip_ref)


def last_kernel(widths, own_ref, back_ref, vectors_ref, second_ref, out_ref):
    shape = (2, ATOM, VECS)
    first = vectors_ref[...].reshape(shape) * keep_of(widths, shape, 1)
    third = applied(widths, own_ref, back_ref)
    out = 2.0 * (third - CENTER * second_ref[...].reshape(shape)) - first
    out_ref[...] = out.reshape(2 * ATOM, VECS)


def piece_at(place, i):
    y, xl = i // 2, i % 2
    return 2 * jnp.bitwise_and(y - place[1] + 4, 3) + xl


def direct_kernel(tab, place, x_ref, t_ref, mine_ref, other_ref, held):
    co = place[0]
    for i in range(8):
        held[pl.ds(2 * piece_at(place, i), 2)] = x_ref[i].reshape(2, ATOM, VECS)
    held[AC] = jnp.zeros((ATOM, VECS), BF)

    def product(a, q, n):
        blocks, xs = [], []
        for k in range(n):
            e = tab[a * D_LEN + q + k]
            blocks.append(t_ref[lax.shift_right_logical(e, 6)])
            xs.append(held[jnp.bitwise_and(e, 63)])
        if n == 1:
            left, right = blocks[0], xs[0]
        else:
            left, right = jnp.concatenate(blocks, 1), jnp.concatenate(xs, 0)
        return jnp.dot(left, right, preferred_element_type=F32)

    def step(xz, carry):
        for which, out in ((0, mine_ref), (1, other_ref)):
            for t in range(2):
                a = 4 * xz + 2 * (co if which == 0 else 1 - co) + t
                total = product(a, 0, 8)
                if t:
                    total = total + product(a, 8, 1)
                out[xz, t * ATOM:(t + 1) * ATOM, :] = total.astype(out.dtype)
        return carry

    lax.fori_loop(0, 8, step, 0, unroll=True)


def mirror_kernel(tab, place, x_ref, y_ref, t_ref, out_ref, held):
    co = place[0]
    for xz in range(8):
        held[pl.ds(4 * xz + 2 * co, 2)] = x_ref[xz]
        held[pl.ds(4 * xz + 2 - 2 * co, 2)] = y_ref[xz]
    held[AR] = jnp.zeros((VECS, ATOM), BF)

    def product(b, q, n):
        blocks, xs = [], []
        for k in range(n):
            e = tab[b * M_LEN + q + k]
            blocks.append(t_ref[lax.shift_right_logical(e, 6)])
            xs.append(held[jnp.bitwise_and(e, 63)])
        if n == 1:
            left, right = xs[0], blocks[0]
        else:
            left, right = jnp.concatenate(xs, 1), jnp.concatenate(blocks, 0)
        return jnp.dot(left, right, preferred_element_type=F32)

    def step(i, carry):
        k = piece_at(place, i)
        for t in range(2):
            b = 2 * k + t
            total = product(b, 0, 8) + product(b, 8, 8)
            if not t:
                total = total + product(b, 16, 1)
            out_ref[i, t] = total.astype(out_ref.dtype)
        return carry

    lax.fori_loop(0, 8, step, 0, unroll=True)


def gathered_kernel(got_ref, out_ref):
    total = got_ref[0].astype(F32)
    for i in range(1, 8):
        total = total + got_ref[i].astype(F32)
    out_ref[...] = total.astype(out_ref.dtype)


def turned_kernel(sum_ref, out_ref):
    out_ref[...] = jnp.swapaxes(sum_ref[...].astype(F32), 1, 2).reshape(2 * ATOM, VECS)


def both_kernel(mine_ref, theirs_ref, out_ref):
    out_ref[...] = (mine_ref[...] + theirs_ref[...].astype(F32)).astype(BF)


SMEM = pl.BlockSpec(memory_space=pltpu.SMEM)
VMEM = pl.BlockSpec(memory_space=pltpu.VMEM)
PARAMS = pltpu.CompilerParams(vmem_limit_bytes=24 * 1024 * 1024)
PIECE = (2 * ATOM, VECS)
BLOCKS = (2, ATOM, VECS)


def like(shape, dtype):
    return jax.ShapeDtypeStruct(shape, dtype)


def call(kernel, out_shape, scalars, arrays, scratch=(), flops=0, size=2**20, name=None):
    single = not isinstance(out_shape, tuple)
    return pl.pallas_call(
        kernel,
        out_shape=out_shape,
        in_specs=[SMEM] * len(scalars) + [VMEM] * len(arrays),
        out_specs=VMEM if single else (VMEM,) * len(out_shape),
        scratch_shapes=list(scratch),
        compiler_params=PARAMS,
        cost_estimate=pl.CostEstimate(flops=flops, bytes_accessed=size, transcendentals=0),
        name=name,
    )(*scalars, *arrays)


def shift_of(column):
    r = column // 2
    return (r // 2 - r % 4 + 2 * (column % 2)) % 4


def owners(r, c):
    column = 2 * r + c // 8
    y, xl = (c % 8 // 2 + shift_of(column)) % 4, c % 2
    return (2 * y + xl) * 16 + column


TO_COL = [(r * 16 + c, owners(r, c)) for r in range(8) for c in range(16)]
TO_ROW = [(d, s) for s, d in TO_COL]
SWAP = [(0, 1), (1, 0)]


def local(vectors, widths, tiles, block_rows, block_cols, block_count):
    row = lax.axis_index(ROWS)
    col = lax.axis_index(COLS)
    place = jnp.stack([lax.axis_index("co"), shift_of(col)]).astype(jnp.int32)
    tile_set = tiles[0, 0]
    direct_tab, mirror_tab = tables(
        block_rows[0, 0], block_cols[0, 0], block_count[0, 0], row, col
    )
    work = dict(flops=2 * SLOTS * ATOM**3, size=2**23)

    def exchange(x, axes):
        return lax.all_to_all(x, axes, split_axis=0, concat_axis=0, tiled=True)

    def apply_matrix(plain, flipped):
        piece = lax.ppermute(plain, ALL, TO_COL)
        near = exchange(flipped, ("xh", "z"))
        piece, near = lax.optimization_barrier((piece, near))
        far = lax.ppermute(near, "co", SWAP)
        col_block = exchange(jnp.broadcast_to(piece[None], (8, *PIECE)), ROWS)
        mirror = call(
            mirror_kernel,
            like((8, *BLOCKS), BF),
            (mirror_tab, place),
            (near, far, tile_set),
            [pltpu.VMEM((AR + 1, VECS, ATOM), BF)],
            name="mirror",
            **work,
        )
        col_block, mirror = lax.optimization_barrier((col_block, mirror))
        got = exchange(mirror, ROWS)
        mine, other = call(
            direct_kernel,
            (like((8, *PIECE), F32), like((8, *PIECE), BF)),
            (direct_tab, place),
            (col_block, tile_set),
            [pltpu.VMEM((AC + 1, ATOM, VECS), BF)],
            name="direct",
            **work,
        )
        other, got = lax.optimization_barrier((other, got))
        theirs = lax.ppermute(other, "co", SWAP)
        both = call(both_kernel, like((8, *PIECE), BF), (), (mine, theirs), name="both")
        own = exchange(both, ("xh", "z"))
        gathered = call(gathered_kernel, like(BLOCKS, BF), (), (got,), name="gathered")
        back = lax.ppermute(gathered, ALL, TO_ROW)
        turned = call(turned_kernel, like(PIECE, F32), (), (back,), name="turned")
        return own, turned

    forms = (like(PIECE, BF), like((8, *BLOCKS), BF))
    plain, flipped = pl.pallas_call(
        first_kernel,
        out_shape=forms,
        in_specs=[pl.BlockSpec(memory_space=pl.ANY)] * 2,
        out_specs=(VMEM, VMEM),
        scratch_shapes=[
            pltpu.SMEM((2,), jnp.int32),
            pltpu.VMEM(PIECE, F32),
            pltpu.SemaphoreType.DMA((2,)),
        ],
        compiler_params=pltpu.CompilerParams(vmem_limit_bytes=56 * 1024 * 1024),
        name="first",
    )(widths, vectors)
    parts = apply_matrix(plain, flipped)
    second, plain, flipped = call(
        second_kernel, (like(PIECE, F32), *forms), (widths,), (*parts, vectors), name="second"
    )
    parts = apply_matrix(plain, flipped)
    return call(
        last_kernel, like(PIECE, F32), (widths,), (*parts, vectors, second), name="last"
    )

def solution(mesh):
    split = Mesh(mesh.devices.reshape(4, 2, 2, 4, 2), ALL)
    return jax.shard_map(
        local,
        mesh=split,
        in_specs=(
            P(ALL, None),
            P(ALL),
            P(ROWS, COLS, None, None, None),
            P(ROWS, COLS, None),
            P(ROWS, COLS, None),
            P(ROWS, COLS),
        ),
        out_specs=P(ALL, None),
        check_vma=False,
    )
```

```python
import functools

import jax
import jax.numpy as jnp
from jax import lax
from jax.experimental import pallas as pl
from jax.experimental.pallas import tpu as pltpu
from jax.sharding import Mesh
from jax.sharding import PartitionSpec as P

CENTER = 0.25
ATOM = 128
VECS = 128
AR = 32
AC = 16
SLOTS = 256
N_ROW = 8
N_COL = 16
BF = jnp.bfloat16
F32 = jnp.float32
ROWS = ("y", "xl")
COLS = ("xh", "z", "co")
ALL = ROWS + COLS
D_LEN = 9
M_LEN = 17


def tables(slot_rows, slot_cols, count, row, col):
    place = jnp.where(jnp.arange(SLOTS) < count, slot_rows * AC + slot_cols, -1)

    def pack(rows, cols, index, zero):
        want = (rows * AC + cols).reshape(-1, 1)
        entry = jnp.arange(SLOTS)[None, :] * 64 + index.reshape(-1, 1) - zero
        return zero + jnp.sum(jnp.where(place[None, :] == want, entry, 0), axis=1)

    a = jnp.arange(AR)[:, None]
    q = jnp.arange(D_LEN)[None, :]
    ga = row * AR + a
    gb = col * AC + 2 * q
    odd = ga % 2 == 1
    main = 2 * q + jnp.where(odd, ga <= gb + 1, ga > gb).astype(jnp.int32)
    extra = ga - 1 - col * AC
    extra = jnp.where(odd & (extra >= 0) & (extra < AC), extra, -AC * AR)
    b = jnp.where(q < 8, main, extra)
    direct = pack(a + 0 * b, b, b, AC)

    b = jnp.arange(AC)[:, None]
    q = jnp.arange(M_LEN)[None, :]
    gb = col * AC + b
    ga = row * AR + 2 * q
    odd = gb % 2 == 1
    main = 2 * q + jnp.where(odd, ga + 1 <= gb, ga > gb).astype(jnp.int32)
    extra = gb + 1 - row * AR
    extra = jnp.where((~odd) & (extra >= 0) & (extra < AR), extra, -AR)
    a = jnp.where(q < 16, main, extra)
    mirror = pack(a, b + 0 * a, a, AR)
    return direct, mirror


def keep_of(widths, shape, axis):
    place = lax.broadcasted_iota(jnp.int32, shape, axis)
    atom = lax.broadcasted_iota(jnp.int32, shape, 0)
    return (place < jnp.where(atom == 0, widths[0], widths[1])).astype(F32)


def send_forms(current, plain_ref, flip_ref):
    plain_ref[...] = current.reshape(2 * ATOM, VECS).astype(BF)
    flipped = jnp.swapaxes(current, 1, 2).astype(BF)
    for k in range(8):
        flip_ref[k] = flipped


def first_kernel(
    widths_ref, vectors_ref, plain_ref, flip_ref, keep_ref, widths, vectors, sem
):
    copies = [
        pltpu.make_async_copy(vectors_ref, vectors, sem.at[0]),
        pltpu.make_async_copy(widths_ref, widths, sem.at[1]),
    ]
    for copy in copies:
        copy.start()
    for copy in copies:
        copy.wait()
    shape = (2, ATOM, VECS)
    keep = keep_of(widths, shape, 1)
    keep_ref[...] = keep
    first = vectors[...].reshape(shape) * keep
    send_forms(first, plain_ref, flip_ref)


def applied(keep_ref, own_ref, back_ref):
    shape = (2, ATOM, VECS)
    total = back_ref[...]
    for k in range(8):
        total = total + own_ref[k].astype(F32)
    return total.reshape(shape) * keep_ref[...]


def second_kernel(keep_ref, own_ref, back_ref, vectors_ref, out_ref, plain_ref, flip_ref):
    shape = (2, ATOM, VECS)
    first = vectors_ref[...].reshape(shape) * keep_ref[...]
    second = applied(keep_ref, own_ref, back_ref) - CENTER * first
    out_ref[...] = second.reshape(2 * ATOM, VECS)
    send_forms(second, plain_ref, flip_ref)


def last_kernel(keep_ref, own_ref, back_ref, vectors_ref, second_ref, out_ref):
    shape = (2, ATOM, VECS)
    first = vectors_ref[...].reshape(shape) * keep_ref[...]
    third = applied(keep_ref, own_ref, back_ref)
    out = 2.0 * (third - CENTER * second_ref[...].reshape(shape)) - first
    out_ref[...] = out.reshape(2 * ATOM, VECS)


def piece_at(place, i):
    y, xl = i // 2, i % 2
    return 2 * jnp.bitwise_and(y - place[1] + 4, 3) + xl


def direct_kernel(tab, place, x_ref, t_ref, mine_ref, other_ref, held):
    co = place[0]
    for i in range(8):
        held[pl.ds(2 * piece_at(place, i), 2)] = x_ref[i].reshape(2, ATOM, VECS)
    held[AC] = jnp.zeros((ATOM, VECS), BF)

    def product(a, q, n):
        blocks, xs = [], []
        for k in range(n):
            e = tab[a * D_LEN + q + k]
            blocks.append(t_ref[lax.shift_right_logical(e, 6)])
            xs.append(held[jnp.bitwise_and(e, 63)])
        if n == 1:
            left, right = blocks[0], xs[0]
        else:
            left, right = jnp.concatenate(blocks, 1), jnp.concatenate(xs, 0)
        return jnp.dot(left, right, preferred_element_type=F32)

    def step(xz, carry):
        for which, out in ((0, mine_ref), (1, other_ref)):
            for t in range(2):
                a = 4 * xz + 2 * (co if which == 0 else 1 - co) + t
                total = product(a, 0, 8)
                if t:
                    total = total + product(a, 8, 1)
                out[xz, t * ATOM:(t + 1) * ATOM, :] = total.astype(out.dtype)
        return carry

    lax.fori_loop(0, 8, step, 0, unroll=True)


def mirror_kernel(tab, place, x_ref, y_ref, t_ref, out_ref, held):
    co = place[0]
    for xz in range(8):
        held[pl.ds(4 * xz + 2 * co, 2)] = x_ref[xz]
        held[pl.ds(4 * xz + 2 - 2 * co, 2)] = y_ref[xz]
    held[AR] = jnp.zeros((VECS, ATOM), BF)

    def product(b, q, n):
        blocks, xs = [], []
        for k in range(n):
            e = tab[b * M_LEN + q + k]
            blocks.append(t_ref[lax.shift_right_logical(e, 6)])
            xs.append(held[jnp.bitwise_and(e, 63)])
        if n == 1:
            left, right = xs[0], blocks[0]
        else:
            left, right = jnp.concatenate(xs, 1), jnp.concatenate(blocks, 0)
        return jnp.dot(left, right, preferred_element_type=F32)

    def step(i, carry):
        k = piece_at(place, i)
        for t in range(2):
            b = 2 * k + t
            total = product(b, 0, 8) + product(b, 8, 8)
            if not t:
                total = total + product(b, 16, 1)
            out_ref[i, t] = total.astype(out_ref.dtype)
        return carry

    lax.fori_loop(0, 8, step, 0, unroll=True)


def gathered_kernel(got_ref, out_ref):
    total = got_ref[0].astype(F32)
    for i in range(1, 8):
        total = total + got_ref[i].astype(F32)
    out_ref[...] = total.astype(out_ref.dtype)


def turned_kernel(sum_ref, out_ref):
    out_ref[...] = jnp.swapaxes(sum_ref[...].astype(F32), 1, 2).reshape(2 * ATOM, VECS)


def both_kernel(mine_ref, theirs_ref, out_ref):
    out_ref[...] = (mine_ref[...] + theirs_ref[...].astype(F32)).astype(BF)


SMEM = pl.BlockSpec(memory_space=pltpu.SMEM)
VMEM = pl.BlockSpec(memory_space=pltpu.VMEM)
PARAMS = pltpu.CompilerParams(vmem_limit_bytes=24 * 1024 * 1024)
PIECE = (2 * ATOM, VECS)
BLOCKS = (2, ATOM, VECS)


def like(shape, dtype):
    return jax.ShapeDtypeStruct(shape, dtype)


def call(kernel, out_shape, scalars, arrays, scratch=(), flops=0, size=2**20, name=None):
    single = not isinstance(out_shape, tuple)
    return pl.pallas_call(
        kernel,
        out_shape=out_shape,
        in_specs=[SMEM] * len(scalars) + [VMEM] * len(arrays),
        out_specs=VMEM if single else (VMEM,) * len(out_shape),
        scratch_shapes=list(scratch),
        compiler_params=PARAMS,
        cost_estimate=pl.CostEstimate(flops=flops, bytes_accessed=size, transcendentals=0),
        name=name,
    )(*scalars, *arrays)


def shift_of(column):
    r = column // 2
    return (r // 2 - r % 4 + 2 * (column % 2)) % 4


def owners(r, c):
    column = 2 * r + c // 8
    y, xl = (c % 8 // 2 + shift_of(column)) % 4, c % 2
    return (2 * y + xl) * 16 + column


TO_COL = [(r * 16 + c, owners(r, c)) for r in range(8) for c in range(16)]
TO_ROW = [(d, s) for s, d in TO_COL]
SWAP = [(0, 1), (1, 0)]


def local(vectors, widths, tiles, block_rows, block_cols, block_count):
    row = lax.axis_index(ROWS)
    col = lax.axis_index(COLS)
    place = jnp.stack([lax.axis_index("co"), shift_of(col)]).astype(jnp.int32)
    tile_set = tiles[0, 0]
    direct_tab, mirror_tab = tables(
        block_rows[0, 0], block_cols[0, 0], block_count[0, 0], row, col
    )
    work = dict(flops=2 * SLOTS * ATOM**3, size=2**23)

    def exchange(x, axes):
        return lax.all_to_all(x, axes, split_axis=0, concat_axis=0, tiled=True)

    def apply_matrix(plain, flipped):
        piece = lax.ppermute(plain, ALL, TO_COL)
        near = exchange(flipped, ("xh", "z"))
        piece, near = lax.optimization_barrier((piece, near))
        far = lax.ppermute(near, "co", SWAP)
        col_block = exchange(jnp.broadcast_to(piece[None], (8, *PIECE)), ROWS)
        mirror = call(
            mirror_kernel,
            like((8, *BLOCKS), BF),
            (mirror_tab, place),
            (near, far, tile_set),
            [pltpu.VMEM((AR + 1, VECS, ATOM), BF)],
            name="mirror",
            **work,
        )
        col_block, mirror = lax.optimization_barrier((col_block, mirror))
        got = exchange(mirror, ROWS)
        mine, other = call(
            direct_kernel,
            (like((8, *PIECE), F32), like((8, *PIECE), BF)),
            (direct_tab, place),
            (col_block, tile_set),
            [pltpu.VMEM((AC + 1, ATOM, VECS), BF)],
            name="direct",
            **work,
        )
        other, got = lax.optimization_barrier((other, got))
        theirs = lax.ppermute(other, "co", SWAP)
        both = call(both_kernel, like((8, *PIECE), BF), (), (mine, theirs), name="both")
        own = exchange(both, ("xh", "z"))
        gathered = call(gathered_kernel, like(BLOCKS, BF), (), (got,), name="gathered")
        back = lax.ppermute(gathered, ALL, TO_ROW)
        turned = call(turned_kernel, like(PIECE, F32), (), (back,), name="turned")
        return own, turned

    forms = (like(PIECE, BF), like((8, *BLOCKS), BF))
    plain, flipped, keep = pl.pallas_call(
        first_kernel,
        out_shape=(*forms, like((2, ATOM, VECS), F32)),
        in_specs=[pl.BlockSpec(memory_space=pl.ANY)] * 2,
        out_specs=(VMEM,) * 3,
        scratch_shapes=[
            pltpu.SMEM((2,), jnp.int32),
            pltpu.VMEM(PIECE, F32),
            pltpu.SemaphoreType.DMA((2,)),
        ],
        compiler_params=pltpu.CompilerParams(vmem_limit_bytes=56 * 1024 * 1024),
        name="first",
    )(widths, vectors)
    parts = apply_matrix(plain, flipped)
    second, plain, flipped = call(
        second_kernel, (like(PIECE, F32), *forms), (), (keep, *parts, vectors), name="second"
    )
    parts = apply_matrix(plain, flipped)
    return call(
        last_kernel, like(PIECE, F32), (), (keep, *parts, vectors, second), name="last"
    )

def solution(mesh):
    split = Mesh(mesh.devices.reshape(4, 2, 2, 4, 2), ALL)
    return jax.shard_map(
        local,
        mesh=split,
        in_specs=(
            P(ALL, None),
            P(ALL),
            P(ROWS, COLS, None, None, None),
            P(ROWS, COLS, None),
            P(ROWS, COLS, None),
            P(ROWS, COLS),
        ),
        out_specs=P(ALL, None),
        check_vma=False,
    )
```

```python
import functools

import jax
import jax.numpy as jnp
from jax import lax
from jax.experimental import pallas as pl
from jax.experimental.pallas import tpu as pltpu
from jax.sharding import Mesh
from jax.sharding import PartitionSpec as P

CENTER = 0.25
ATOM = 128
VECS = 128
AR = 32
AC = 16
SLOTS = 256
N_ROW = 8
N_COL = 16
BF = jnp.bfloat16
F32 = jnp.float32
ROWS = ("y", "xl")
COLS = ("xh", "z", "co")
ALL = ROWS + COLS
D_LEN = 9
M_LEN = 17


def tables(slot_rows, slot_cols, count, row, col):
    place = jnp.where(jnp.arange(SLOTS) < count, slot_rows * AC + slot_cols, -1)

    def pack(rows, cols, index, zero):
        want = (rows * AC + cols).reshape(-1, 1)
        entry = jnp.arange(SLOTS)[None, :] * 64 + index.reshape(-1, 1) - zero
        return zero + jnp.sum(jnp.where(place[None, :] == want, entry, 0), axis=1)

    a = jnp.arange(AR)[:, None]
    q = jnp.arange(D_LEN)[None, :]
    ga = row * AR + a
    gb = col * AC + 2 * q
    odd = ga % 2 == 1
    main = 2 * q + jnp.where(odd, ga <= gb + 1, ga > gb).astype(jnp.int32)
    extra = ga - 1 - col * AC
    extra = jnp.where(odd & (extra >= 0) & (extra < AC), extra, -AC * AR)
    b = jnp.where(q < 8, main, extra)
    direct = pack(a + 0 * b, b, b, AC)

    b = jnp.arange(AC)[:, None]
    q = jnp.arange(M_LEN)[None, :]
    gb = col * AC + b
    ga = row * AR + 2 * q
    odd = gb % 2 == 1
    main = 2 * q + jnp.where(odd, ga + 1 <= gb, ga > gb).astype(jnp.int32)
    extra = gb + 1 - row * AR
    extra = jnp.where((~odd) & (extra >= 0) & (extra < AR), extra, -AR)
    a = jnp.where(q < 16, main, extra)
    mirror = pack(a, b + 0 * a, a, AR)
    return direct, mirror


def keep_of(widths, shape, axis):
    place = lax.broadcasted_iota(jnp.int32, shape, axis)
    atom = lax.broadcasted_iota(jnp.int32, shape, 0)
    return (place < jnp.where(atom == 0, widths[0], widths[1])).astype(F32)


def send_forms(current, plain_ref, flip_ref):
    plain_ref[...] = current.reshape(2 * ATOM, VECS).astype(BF)
    flipped = jnp.swapaxes(current, 1, 2).astype(BF)
    for k in range(8):
        flip_ref[k] = flipped


def first_kernel(
    widths_ref, vectors_ref, plain_ref, flip_ref, keep_ref, widths, vectors, sem
):
    copies = [
        pltpu.make_async_copy(vectors_ref, vectors, sem.at[0]),
        pltpu.make_async_copy(widths_ref, widths, sem.at[1]),
    ]
    for copy in copies:
        copy.start()
    for copy in copies:
        copy.wait()
    shape = (2, ATOM, VECS)
    keep = keep_of(widths, shape, 1)
    keep_ref[...] = keep
    first = vectors[...].reshape(shape) * keep
    send_forms(first, plain_ref, flip_ref)


def applied(keep_ref, own_ref, back_ref):
    shape = (2, ATOM, VECS)
    total = back_ref[...]
    for k in range(8):
        total = total + own_ref[k].astype(F32)
    return total.reshape(shape) * keep_ref[...]


def second_kernel(keep_ref, own_ref, back_ref, vectors_ref, out_ref, plain_ref, flip_ref):
    shape = (2, ATOM, VECS)
    first = vectors_ref[...].reshape(shape) * keep_ref[...]
    second = applied(keep_ref, own_ref, back_ref) - CENTER * first
    out_ref[...] = second.reshape(2 * ATOM, VECS)
    send_forms(second, plain_ref, flip_ref)


def last_kernel(keep_ref, own_ref, back_ref, vectors_ref, second_ref, out_ref):
    shape = (2, ATOM, VECS)
    first = vectors_ref[...].reshape(shape) * keep_ref[...]
    third = applied(keep_ref, own_ref, back_ref)
    out = 2.0 * (third - CENTER * second_ref[...].reshape(shape)) - first
    out_ref[...] = out.reshape(2 * ATOM, VECS)


def piece_at(place, i):
    y, xl = i // 2, i % 2
    return 2 * jnp.bitwise_and(y - place[1] + 4, 3) + xl


def direct_kernel(tab, place, x_ref, t_ref, mine_ref, other_ref, held):
    co = place[0]
    for i in range(8):
        held[pl.ds(2 * piece_at(place, i), 2)] = x_ref[i].reshape(2, ATOM, VECS)
    held[AC] = jnp.zeros((ATOM, VECS), BF)

    def product(a, q, n):
        blocks, xs = [], []
        for k in range(n):
            e = tab[a * D_LEN + q + k]
            blocks.append(t_ref[lax.shift_right_logical(e, 6)])
            xs.append(held[jnp.bitwise_and(e, 63)])
        if n == 1:
            left, right = blocks[0], xs[0]
        else:
            left, right = jnp.concatenate(blocks, 1), jnp.concatenate(xs, 0)
        return jnp.dot(left, right, preferred_element_type=F32)

    def step(xz, carry):
        for which, out in ((0, mine_ref), (1, other_ref)):
            for t in range(2):
                a = 4 * xz + 2 * (co if which == 0 else 1 - co) + t
                total = product(a, 0, 8)
                if t:
                    total = total + product(a, 8, 1)
                out[xz, t * ATOM:(t + 1) * ATOM, :] = total.astype(out.dtype)
        return carry

    lax.fori_loop(0, 8, step, 0, unroll=True)


def mirror_kernel(tab, place, x_ref, y_ref, t_ref, out_ref, held):
    co = place[0]
    for xz in range(8):
        held[pl.ds(4 * xz + 2 * co, 2)] = x_ref[xz]
        held[pl.ds(4 * xz + 2 - 2 * co, 2)] = y_ref[xz]
    held[AR] = jnp.zeros((VECS, ATOM), BF)

    def product(b, q, n):
        blocks, xs = [], []
        for k in range(n):
            e = tab[b * M_LEN + q + k]
            blocks.append(t_ref[lax.shift_right_logical(e, 6)])
            xs.append(held[jnp.bitwise_and(e, 63)])
        if n == 1:
            left, right = xs[0], blocks[0]
        else:
            left, right = jnp.concatenate(xs, 1), jnp.concatenate(blocks, 0)
        return jnp.dot(left, right, preferred_element_type=F32)

    def step(i, carry):
        k = piece_at(place, i)
        for t in range(2):
            b = 2 * k + t
            total = product(b, 0, 8) + product(b, 8, 8)
            if not t:
                total = total + product(b, 16, 1)
            out_ref[i, t] = total.astype(out_ref.dtype)
        return carry

    lax.fori_loop(0, 8, step, 0, unroll=True)


def gathered_kernel(got_ref, out_ref):
    total = got_ref[0].astype(F32)
    for i in range(1, 8):
        total = total + got_ref[i].astype(F32)
    out_ref[...] = total.astype(out_ref.dtype)


def turned_kernel(sum_ref, out_ref):
    out_ref[...] = jnp.swapaxes(sum_ref[...].astype(F32), 1, 2).reshape(2 * ATOM, VECS)


def both_kernel(mine_ref, theirs_ref, out_ref):
    out_ref[...] = (mine_ref[...] + theirs_ref[...].astype(F32)).astype(BF)


SMEM = pl.BlockSpec(memory_space=pltpu.SMEM)
VMEM = pl.BlockSpec(memory_space=pltpu.VMEM)
PARAMS = pltpu.CompilerParams(vmem_limit_bytes=24 * 1024 * 1024)
PIECE = (2 * ATOM, VECS)
BLOCKS = (2, ATOM, VECS)


def like(shape, dtype):
    return jax.ShapeDtypeStruct(shape, dtype)


def call(kernel, out_shape, scalars, arrays, scratch=(), flops=0, size=2**20, name=None):
    single = not isinstance(out_shape, tuple)
    return pl.pallas_call(
        kernel,
        out_shape=out_shape,
        in_specs=[SMEM] * len(scalars) + [VMEM] * len(arrays),
        out_specs=VMEM if single else (VMEM,) * len(out_shape),
        scratch_shapes=list(scratch),
        compiler_params=PARAMS,
        cost_estimate=pl.CostEstimate(flops=flops, bytes_accessed=size, transcendentals=0),
        name=name,
    )(*scalars, *arrays)


def shift_of(column):
    r = column // 2
    return (r // 2 + 2 * (column % 2)) % 4


def owners(r, c):
    column = 2 * r + c // 8
    y, xl = (c % 8 // 2 + shift_of(column)) % 4, c % 2
    return (2 * y + xl) * 16 + column


TO_COL = [(r * 16 + c, owners(r, c)) for r in range(8) for c in range(16)]
TO_ROW = [(d, s) for s, d in TO_COL]
SWAP = [(0, 1), (1, 0)]


def local(vectors, widths, tiles, block_rows, block_cols, block_count):
    row = lax.axis_index(ROWS)
    col = lax.axis_index(COLS)
    place = jnp.stack([lax.axis_index("co"), shift_of(col)]).astype(jnp.int32)
    tile_set = tiles[0, 0]
    direct_tab, mirror_tab = tables(
        block_rows[0, 0], block_cols[0, 0], block_count[0, 0], row, col
    )
    work = dict(flops=2 * SLOTS * ATOM**3, size=2**23)

    def exchange(x, axes):
        return lax.all_to_all(x, axes, split_axis=0, concat_axis=0, tiled=True)

    def apply_matrix(plain, flipped):
        piece = lax.ppermute(plain, ALL, TO_COL)
        near = exchange(flipped, ("xh", "z"))
        piece, near = lax.optimization_barrier((piece, near))
        far = lax.ppermute(near, "co", SWAP)
        col_block = exchange(jnp.broadcast_to(piece[None], (8, *PIECE)), ROWS)
        mirror = call(
            mirror_kernel,
            like((8, *BLOCKS), BF),
            (mirror_tab, place),
            (near, far, tile_set),
            [pltpu.VMEM((AR + 1, VECS, ATOM), BF)],
            name="mirror",
            **work,
        )
        col_block, mirror = lax.optimization_barrier((col_block, mirror))
        got = exchange(mirror, ROWS)
        mine, other = call(
            direct_kernel,
            (like((8, *PIECE), F32), like((8, *PIECE), BF)),
            (direct_tab, place),
            (col_block, tile_set),
            [pltpu.VMEM((AC + 1, ATOM, VECS), BF)],
            name="direct",
            **work,
        )
        other, got = lax.optimization_barrier((other, got))
        theirs = lax.ppermute(other, "co", SWAP)
        both = call(both_kernel, like((8, *PIECE), BF), (), (mine, theirs), name="both")
        own = exchange(both, ("xh", "z"))
        gathered = call(gathered_kernel, like(BLOCKS, BF), (), (got,), name="gathered")
        back = lax.ppermute(gathered, ALL, TO_ROW)
        turned = call(turned_kernel, like(PIECE, F32), (), (back,), name="turned")
        return own, turned

    forms = (like(PIECE, BF), like((8, *BLOCKS), BF))
    plain, flipped, keep = pl.pallas_call(
        first_kernel,
        out_shape=(*forms, like((2, ATOM, VECS), F32)),
        in_specs=[pl.BlockSpec(memory_space=pl.ANY)] * 2,
        out_specs=(VMEM,) * 3,
        scratch_shapes=[
            pltpu.SMEM((2,), jnp.int32),
            pltpu.VMEM(PIECE, F32),
            pltpu.SemaphoreType.DMA((2,)),
        ],
        compiler_params=pltpu.CompilerParams(vmem_limit_bytes=56 * 1024 * 1024),
        name="first",
    )(widths, vectors)
    parts = apply_matrix(plain, flipped)
    second, plain, flipped = call(
        second_kernel, (like(PIECE, F32), *forms), (), (keep, *parts, vectors), name="second"
    )
    parts = apply_matrix(plain, flipped)
    return call(
        last_kernel, like(PIECE, F32), (), (keep, *parts, vectors, second), name="last"
    )

def solution(mesh):
    split = Mesh(mesh.devices.reshape(4, 2, 2, 4, 2), ALL)
    return jax.shard_map(
        local,
        mesh=split,
        in_specs=(
            P(ALL, None),
            P(ALL),
            P(ROWS, COLS, None, None, None),
            P(ROWS, COLS, None),
            P(ROWS, COLS, None),
            P(ROWS, COLS),
        ),
        out_specs=P(ALL, None),
        check_vma=False,
    )
```
